256 devices in a mesh: blk: 32 (over y, z), col: 8 (over x, core).
Axes of the slice: x: 4, y: 4, z: 8, core: 2. Of those that a mesh axis runs over, the one named last changes fastest.
Arguments:
- right_side: float32 [64, 2048, 128], P('blk'), may hold values from -6 to 6
- below_blocks: float32 [64, 3, 128, 2048], P('blk', None, None, 'col'), may hold values from -0.09375 to 0.09375
- diag_cols: float32 [64, 2048, 128], P('blk', 'col'), as said below
- tile_home: int32 [48], replicated, may hold values from 0 to 63, as said below
- block_rows: int32 [3, 32], replicated, may hold values from 0 to 47, as said below
- block_counts: int32 [3], replicated, may hold values from 0 to 32, as said below
Outputs:
- solution: float32 [64, 2048, 128], P('blk', 'col')
The draws below stay inside these ranges and needn't reach their ends.
Inputs may be any that keep to these rules, and one draw needn't show every extreme that they name: `tile_home`: distinct slots. For each supernode s, entries 0 to block_counts[s] - 1 of block_rows[s] are distinct tiles of supernodes after s; the remaining entries are arbitrary tiles. block_counts[0] is 32, block_counts[2] is 0, and block_counts[s] is at most (2 - s) * 16. For a tile t, diag_cols[tile_home[t]] is zero at rows i and columns j with i < (t % 16) * 128 + j.
All inputs are finite; a program needn't handle non-finite values.
Results may differ from the reference program's by a relative error of at most 0.0001.
Values sent between devices are 32-bit elements; how exact they have to be, the bound alone decides.
A program may use at most 64 MiB of HBM per device.

```python
import math
import jax
import jax.numpy as jnp
from jax import lax

TILE = 128
WIDTH = 2048
SUPERS = 3
SAMPLES = 2048
TILES_SUP = 16
TILES = 48
MAX_BELOW = 32
SLOTS = 64


def home_slots(key):
    return jax.random.permutation(jax.random.fold_in(key, 11), SLOTS)[:TILES].astype(jnp.int32)


def draw_tile_home(key, part):
    return home_slots(key)


def draw_diag_cols(key, part):
    home_map = home_slots(key)
    tile_at = jnp.zeros((SLOTS,), jnp.int32).at[home_map].set(jnp.arange(TILES, dtype=jnp.int32))
    within = tile_at % TILES_SUP
    row_ids = jnp.arange(WIDTH, dtype=jnp.int32)[None, :, None]
    col_ids = within[:, None, None] * TILE + jnp.arange(TILE, dtype=jnp.int32)[None, None, :]
    key_main, key_diag = jax.random.split(jax.random.fold_in(key, 23))
    noise_part = jax.random.normal(key_main, (SLOTS, WIDTH, TILE), jnp.float32)
    scales = jax.random.uniform(key_diag, (SLOTS, WIDTH, TILE), jnp.float32, 0.6, 1.6)
    lower_part = (row_ids > col_ids).astype(jnp.float32) * noise_part * (0.7 / math.sqrt(WIDTH))
    return lower_part + (row_ids == col_ids).astype(jnp.float32) * scales


def draw_block_rows(key, part):
    line_list = []
    for level_now in range(SUPERS):
        later_tiles = (SUPERS - 1 - level_now) * TILES_SUP
        padding = jax.random.randint(jax.random.fold_in(key, 41 + level_now), (MAX_BELOW - later_tiles,), 0, TILES).astype(jnp.int32)
        if later_tiles > 0:
            order_tiles = jax.random.permutation(jax.random.fold_in(key, 61 + level_now), later_tiles).astype(jnp.int32)
            order_tiles = order_tiles + (level_now + 1) * TILES_SUP
            line_list.append(jnp.concatenate([order_tiles, padding]))
        else:
            line_list.append(padding)
    return jnp.stack(line_list)


def draw_block_counts(key, part):
    count_parts = []
    for level_now in range(SUPERS):
        later_tiles = (SUPERS - 1 - level_now) * TILES_SUP
        if level_now == 0:
            count_now = jnp.full((), later_tiles, jnp.int32)
        elif level_now == SUPERS - 1:
            count_now = jnp.zeros((), jnp.int32)
        else:
            count_now = jax.random.randint(jax.random.fold_in(key, 81 + level_now), (), later_tiles // 2, later_tiles + 1).astype(jnp.int32)
        count_parts.append(count_now)
    return jnp.stack(count_parts)


def shard_levels(rng, extent, cuts, least, top_value):
    level = 1.0
    for dim, parts in cuts:
        draws = jax.random.uniform(jax.random.fold_in(jax.random.fold_in(rng, 6), dim), (parts,), jnp.float32, least / len(cuts), top_value / len(cuts))
        level = level * jnp.repeat(jnp.exp(draws), extent[dim] // parts).reshape((-1,) + (1,) * (len(extent) - 1 - dim))
    return level


def gaussian(key, extent, scale, bound, cuts=(), held_as=jnp.bfloat16):
    values = jax.random.normal(key, extent, jnp.float32) * scale
    if len(cuts) > 0:
        values = shard_levels(key, extent, cuts, -0.22, 0.18) * values
    return jnp.clip(values, min=-bound, max=bound).astype(held_as)


def setup_inputs(seed: int = 0) -> dict:
    arg_keys = jax.random.split(jax.random.key(seed), 7)
    right_side = gaussian(arg_keys[0], (SLOTS, SAMPLES, TILE), 1.0, 6.0, ((0, 32),), jnp.float32)
    below_blocks = gaussian(arg_keys[1], (SLOTS, SUPERS, TILE, WIDTH), (MAX_BELOW * TILE) ** -0.5, 0.09375, ((0, 32), (3, 8)), jnp.float32)
    diag_cols = draw_diag_cols(jax.random.fold_in(arg_keys[6], 71), 0)
    tile_home = draw_tile_home(jax.random.fold_in(arg_keys[6], 71), 0)
    block_rows = draw_block_rows(jax.random.fold_in(arg_keys[6], 71), 0)
    block_counts = draw_block_counts(jax.random.fold_in(arg_keys[6], 71), 0)
    return {"right_side": right_side, "below_blocks": below_blocks, "diag_cols": diag_cols, "tile_home": tile_home, "block_rows": block_rows, "block_counts": block_counts}


def reference(right_side, below_blocks, diag_cols, tile_home, block_rows, block_counts):
    precise = lax.Precision.HIGHEST
    tile_ids = jnp.arange(TILES, dtype=jnp.int32)
    live_rows = jnp.arange(MAX_BELOW, dtype=jnp.int32)[None, :] < block_counts[:, None]
    matches = (block_rows[None, :, :] == tile_ids[:, None, None]) & live_rows[None, :, :]
    present = jnp.any(matches, axis=2).astype(jnp.float32)
    solved = jnp.zeros((TILES, SAMPLES, TILE), jnp.float32)
    for level_now in range(SUPERS - 1, -1, -1):
        first_tile = level_now * TILES_SUP
        own_slots = tile_home[first_tile:first_tile + TILES_SUP]
        residual = jnp.transpose(right_side[own_slots], (1, 0, 2)).reshape(SAMPLES, WIDTH)
        if level_now < SUPERS - 1:
            blocks = below_blocks[tile_home, level_now]
            masked = solved * present[:, level_now][:, None, None]
            flat_rows = jnp.transpose(masked, (1, 0, 2)).reshape(SAMPLES, TILES * TILE)
            residual = residual - jnp.dot(flat_rows, blocks.reshape(TILES * TILE, WIDTH), precision=precise, preferred_element_type=jnp.float32)
        inverse = jnp.transpose(diag_cols[own_slots], (1, 0, 2)).reshape(WIDTH, TILES_SUP * TILE)
        new_rows = jnp.dot(residual, inverse, precision=precise, preferred_element_type=jnp.float32)
        new_rows = jnp.transpose(new_rows.reshape(SAMPLES, TILES_SUP, TILE), (1, 0, 2))
        solved = solved.at[first_tile:first_tile + TILES_SUP].set(new_rows)
    return jnp.zeros((SLOTS, SAMPLES, TILE), jnp.float32).at[tile_home].set(solved)
```

```python
import functools

import jax
import jax.numpy as jnp
from jax import lax
from jax.experimental import pallas as pl
from jax.experimental.pallas import tpu as pltpu
from jax.sharding import PartitionSpec as P

TILE = 128
SUPERS = 3
SAMPLES = 2048
TILES_SUP = 16
TILES = 48
MAX_BELOW = 32
NX, NY, NZ = 4, 4, 8
ROWS = 128
HALF = 64
MESH = pl.DeviceIdType.MESH
F32 = jnp.float32
BF16 = jnp.bfloat16


def masks(tile_home, block_rows, block_counts):
    z = lax.axis_index("blk") % NZ
    core = lax.axis_index("col") % 2
    order = jnp.arange(8, dtype=jnp.int32)
    slots = ((order // 2) * NZ + z) * 2 + order % 2
    matched = tile_home[None, :] == slots[:, None]
    tile_of = jnp.max(jnp.where(matched, jnp.arange(TILES, dtype=jnp.int32)[None, :], -1), axis=1)
    levels = jnp.arange(SUPERS, dtype=jnp.int32)
    in_level = (tile_of[None, :] // TILES_SUP == levels[:, None]) & (tile_of >= 0)[None, :]
    cols = 4 * (order // 2) + 2 * core + order % 2
    placing = in_level[:, None, :] & (tile_of % TILES_SUP == cols[:, None])[None, :, :]
    live = jnp.arange(MAX_BELOW, dtype=jnp.int32)[None, :] < block_counts[:, None]
    hits = (block_rows[:, :, None] == tile_of[None, None, :]) & live[:, :, None]
    present = jnp.any(hits, axis=1)
    both = jnp.stack([in_level, present], axis=1)
    return jnp.concatenate([placing, both], axis=1).astype(F32).reshape(SUPERS * 10 * 8)


def split(v):
    hi = v.astype(BF16)
    return hi, (v - hi.astype(F32)).astype(BF16)


def kernel(
    mask, rhs, below, diag, out,
    b8, df0, df1, lf0, lf1, dhi, dlo, lhi, llo, xhi, xlo,
    part, rbuf, chunk, res, spart, exch, exch0, sol, outs, outr,
    send, recv, local,
):
    blk, col = lax.axis_index("blk"), lax.axis_index("col")
    y, z = blk // NZ, blk % NZ
    x, k = col // 2, col % 2
    count = [0, 0]

    def at(dy=0, dz=0, dx=0, dk=0):
        return (((y + dy) % NY) * NZ + (z + dz) % NZ, ((x + dx) % NX) * 2 + (k + dk) % 2)

    def push(src, dst, **where):
        i = count[0]
        count[0] += 1
        c = pltpu.make_async_remote_copy(
            src_ref=src, dst_ref=dst, send_sem=send.at[i], recv_sem=recv.at[i],
            device_id=at(**where), device_id_type=MESH,
        )
        c.start()
        sent.append(c)
        return c

    def keep(src, dst):
        i = count[1]
        count[1] += 1
        c = pltpu.make_async_copy(src, dst, local.at[i])
        c.start()
        return c

    sent = []
    own = [keep(diag.at[0], df0.at[y, x]), keep(diag.at[1], df1.at[x, y])]
    own_b = []
    for h in range(2):
        start = pl.multiple_of((2 * x + h) * 256 + y * HALF, HALF)
        own_b.append(keep(rhs.at[:, pl.ds(start, HALF), :], b8.at[y, :, pl.ds(h * HALF, HALF), :]))
    own_l = []
    for s in (1, 0):
        own_l.append(
            [keep(below.at[0, s], lf0.at[s, y, x]), keep(below.at[1, s], lf1.at[s, x, y])]
        )

    peers = [dict(dy=d) for d in range(1, NY)] + [dict(dx=d) for d in range(1, NX)]
    peers += [dict(dz=d) for d in range(1, NZ)] + [dict(dk=1)]
    barrier = pltpu.get_barrier_semaphore()
    for p in peers:
        pl.semaphore_signal(barrier, inc=1, device_id=at(**p), device_id_type=MESH)
    pl.semaphore_wait(barrier, len(peers))

    bcopies = []
    for d in (1, 3, 2):
        for h in range(2):
            start = pl.multiple_of((2 * x + h) * 256 + ((y + d) % NY) * HALF, HALF)
            bcopies.append(
                push(
                    rhs.at[:, pl.ds(start, HALF), :],
                    b8.at[y, :, pl.ds(h * HALF, HALF), :],
                    dy=d,
                )
            )

    def first(src0, dst0, src1, dst1):
        cs = []
        for d in (1, 3, 2):
            cs.append(push(src0, dst0, dx=d))
            cs.append(push(src1, dst1, dy=d))
        return cs

    def second(src0, src1):
        cs = []
        for d in (1, 3, 2):
            cs.append(push(src0, src0, dy=d))
            cs.append(push(src1, src1, dx=d))
        return cs

    def arrive(cs):
        for c in cs:
            c.wait_recv()

    d_first = first(diag.at[0], df0.at[y, x], diag.at[1], df1.at[x, y])

    for c in own_b:
        c.wait()
    arrive(bcopies)

    def place(s):
        def tile(t, carry):
            acc = jnp.zeros((ROWS, TILE), F32)
            for i in range(8):
                acc = acc + b8[i // 2, i % 2] * mask[(s * 10 + t) * 8 + i]
            part[s, t] = acc
            return carry

        lax.fori_loop(0, 8, tile, 0)

    def scatter(s):
        cs = []
        for d in (4, 3, 5, 2, 6, 1, 7):
            cs.append(push(part.at[s, (z + d) % NZ], rbuf.at[s, d - 1], dz=d))
        return cs

    def reduce(s):
        total = part[s, z]
        for d in range(1, NZ):
            total = total + rbuf[s, d - 1]
        chunk[s] = total
        res[s, z] = total

    def gather(s):
        cs = []
        for d in (4, 3, 5, 2, 6, 1, 7):
            cs.append(push(chunk.at[s], res.at[s, z], dz=d))
        return cs

    place(2)
    rs = scatter(2)

    for c in own:
        c.wait()
    arrive(d_first)
    d_second = second(df0.at[y], df1.at[x])
    l1_first = first(below.at[0, 1], lf0.at[1, y, x], below.at[1, 1], lf1.at[1, x, y])
    place(1)
    place(0)
    arrive(rs)
    reduce(2)
    ag = gather(2)
    arrive(d_second)
    for c in own_l[0]:
        c.wait()
    arrive(l1_first)
    l1_second = second(lf0.at[1, y], lf1.at[1, x])
    l0_first = first(below.at[0, 0], lf0.at[0, y, x], below.at[1, 0], lf1.at[0, x, y])

    def convert_d(i, carry):
        a, b = i // 4, i % 4
        rows = pl.ds(pl.multiple_of(b * 256, 256), 256)
        for j, v in ((0, df0[a, b]), (1, df1[b, a])):
            hi, lo = split(v)
            dhi[a, rows, j * TILE:(j + 1) * TILE] = hi
            dlo[a, rows, j * TILE:(j + 1) * TILE] = lo
        return carry

    def convert_l(s):
        def step(i, carry):
            a, b = i // 4, i % 4
            for j, v in ((0, lf0[s, a, b]), (1, lf1[s, b, a])):
                hi, lo = split(v)
                rows = pl.ds(pl.multiple_of(a * 256 + j * TILE, TILE), TILE)
                lhi[b, rows, :] = hi
                llo[b, rows, :] = lo
            return carry

        lax.fori_loop(0, 16, step, 0)

    def product(whi, wlo, n):
        a, b = xhi[...], xlo[...]
        w = whi[n]
        acc = jnp.dot(a, w, preferred_element_type=F32)
        acc = acc + jnp.dot(b, w, preferred_element_type=F32)
        return acc + jnp.dot(a, wlo[n], preferred_element_type=F32)

    def diag_step(s):
        for t in range(8):
            hi, lo = split(res[s, t])
            xhi[:, t * TILE:(t + 1) * TILE] = hi
            xlo[:, t * TILE:(t + 1) * TILE] = lo

        def step(n, carry):
            spart[s, n] = product(dhi, dlo, n)
            return carry

        lax.fori_loop(0, 4, step, 0)

    def lanes(s, row, n):
        lane = lax.broadcasted_iota(jnp.int32, (1, 256), 1)
        base = (s * 10 + row) * 8 + 2 * n
        return jnp.where(lane < TILE, mask[base], mask[base + 1])

    def absorb(s, target):
        def step(n, carry):
            v = jnp.where(lanes(s, 8, n) > 0.5, spart[s, n] + exch[s, n], 0.0)
            if s < SUPERS - 1:
                v = v + sol[n]
            sol[n] = v
            hi, lo = split(v * lanes(target, 9, n))
            where = pl.ds(pl.multiple_of(n * 256, 256), 256)
            xhi[:, where] = hi
            xlo[:, where] = lo
            return carry

        lax.fori_loop(0, 4, step, 0)

    def below_step(s):
        def step(n, carry):
            acc = product(lhi, llo, n)
            part[s, 2 * n] = part[s, 2 * n] - acc[:, :TILE]
            part[s, 2 * n + 1] = part[s, 2 * n + 1] - acc[:, TILE:]
            return carry

        lax.fori_loop(0, 4, step, 0)

    lax.fori_loop(0, 16, convert_d, 0)
    arrive(ag)
    diag_step(2)
    ex = push(spart.at[2], exch.at[2], dk=1)
    for c in own_l[1]:
        c.wait()
    arrive(l0_first)
    arrive(l1_second)
    l0_second = second(lf0.at[0, y], lf1.at[0, x])
    convert_l(1)
    ex.wait_recv()
    absorb(2, 1)
    below_step(1)
    rs = scatter(1)
    arrive(rs)
    reduce(1)
    ag = gather(1)
    arrive(l0_second)
    convert_l(0)
    arrive(ag)
    diag_step(1)
    ex = push(spart.at[1], exch.at[1], dk=1)
    ex.wait_recv()
    absorb(1, 0)
    below_step(0)
    rs = scatter(0)
    arrive(rs)
    reduce(0)
    ag = gather(0)
    arrive(ag)
    diag_step(0)
    other = pl.ds(pl.multiple_of((1 - k) * HALF, HALF), HALF)
    mine = pl.ds(pl.multiple_of(k * HALF, HALF), HALF)
    ex = push(spart.at[0, :, other, :], exch0, dk=1)
    ex.wait_recv()
    for n in range(4):
        v = spart[0, n, mine, :] + exch0[n]
        v = sol[n, mine, :] + jnp.where(lanes(0, 8, n) > 0.5, v, 0.0)
        outs[n, 0] = v[:, :TILE]
        outs[n, 1] = v[:, TILE:]
    oc = [push(outs.at[(y + d) % NY], outr.at[y], dy=d) for d in (1, 3, 2)]
    outr[y] = outs[y]
    arrive(oc)
    for n in range(4):
        for j in range(2):
            out[j, n * HALF:(n + 1) * HALF, :] = outr[n, j]
    for c in sent:
        c.wait_send()


COPIES = 120


def body(right_side, below_blocks, diag_cols, tile_home, block_rows, block_counts):
    vm = pltpu.VMEM
    anyspace = pl.BlockSpec(memory_space=pl.ANY)
    return pl.pallas_call(
        kernel,
        name="solve",
        out_shape=jax.ShapeDtypeStruct((2, 256, TILE), F32),
        in_specs=[pl.BlockSpec(memory_space=pltpu.SMEM), anyspace, anyspace, anyspace],
        out_specs=pl.BlockSpec(memory_space=pltpu.VMEM),
        scratch_shapes=[
            vm((4, 2, ROWS, TILE), F32),
            vm((4, 4, 256, TILE), F32),
            vm((4, 4, 256, TILE), F32),
            vm((2, 4, 4, TILE, 256), F32),
            vm((2, 4, 4, TILE, 256), F32),
            vm((4, 1024, 256), BF16),
            vm((4, 1024, 256), BF16),
            vm((4, 1024, 256), BF16),
            vm((4, 1024, 256), BF16),
            vm((ROWS, 1024), BF16),
            vm((ROWS, 1024), BF16),
            vm((3, 8, ROWS, TILE), F32),
            vm((3, 7, ROWS, TILE), F32),
            vm((3, ROWS, TILE), F32),
            vm((3, 8, ROWS, TILE), F32),
            vm((3, 4, ROWS, 256), F32),
            vm((3, 4, ROWS, 256), F32),
            vm((4, HALF, 256), F32),
            vm((4, ROWS, 256), F32),
            vm((4, 2, HALF, TILE), F32),
            vm((4, 2, HALF, TILE), F32),
            pltpu.SemaphoreType.DMA((COPIES,)),
            pltpu.SemaphoreType.DMA((COPIES,)),
            pltpu.SemaphoreType.DMA((8,)),
        ],
        compiler_params=pltpu.CompilerParams(
            collective_id=0, has_side_effects=True, vmem_limit_bytes=48 * 2**20
        ),
    )(masks(tile_home, block_rows, block_counts), right_side, below_blocks, diag_cols)


def solution(mesh):
    return jax.shard_map(
        body,
        mesh=mesh,
        in_specs=(
            P("blk", None, None),
            P("blk", None, None, "col"),
            P("blk", "col", None),
            P(),
            P(),
            P(),
        ),
        out_specs=P("blk", "col", None),
        check_vma=False,
    )
```

```python
import jax
import jax.numpy as jnp
from jax import lax
from jax.experimental import pallas as pl
from jax.experimental.pallas import tpu as pltpu
from jax.sharding import PartitionSpec as P

TILE = 128
SUPERS = 3
SAMPLES = 2048
TILES_SUP = 16
TILES = 48
MAX_BELOW = 32
NX, NY, NZ = 4, 4, 8
ROWS = 128
HALF = 64
MESH = pl.DeviceIdType.MESH
F32 = jnp.float32
BF16 = jnp.bfloat16


def split(v):
    hi = v.astype(BF16)
    return hi, (v - hi.astype(F32)).astype(BF16)


def kernel(
    home_in, rows_in, counts_in, rhs, below, diag, out,
    home, rows_ref, counts, mask,
    b8, df0, df1, lf0, lf1, dhi, dlo, lhi, llo, xhi, xlo,
    part, rbuf, chunk, res, spart, exch, exch0, sol, outs, outr,
    send, recv, local,
):
    blk, col = lax.axis_index("blk"), lax.axis_index("col")
    y, z = blk // NZ, blk % NZ
    x, k = col // 2, col % 2
    count = [0, 0]
    other = pl.ds(pl.multiple_of((1 - k) * HALF, HALF), HALF)
    mine = pl.ds(pl.multiple_of(k * HALF, HALF), HALF)

    def at(dy=0, dz=0, dx=0, dk=0):
        return (((y + dy) % NY) * NZ + (z + dz) % NZ, ((x + dx) % NX) * 2 + (k + dk) % 2)

    def push(src, dst, slot=None, **where):
        i = slot
        if slot is None:
            i = count[0]
            count[0] += 1
        c = pltpu.make_async_remote_copy(
            src_ref=src, dst_ref=dst, send_sem=send.at[i], recv_sem=recv.at[i],
            device_id=at(**where), device_id_type=MESH,
        )
        c.start()
        if slot is None:
            sent.append(c)
        return c

    def keep(src, dst):
        i = count[1]
        count[1] += 1
        c = pltpu.make_async_copy(src, dst, local.at[i])
        c.start()
        return c

    sent = []
    ints = [keep(home_in, home), keep(rows_in, rows_ref), keep(counts_in, counts)]
    own = [keep(diag.at[0], df0.at[y, x]), keep(diag.at[1], df1.at[x, y])]
    own_b = []
    for h in range(2):
        start = pl.multiple_of((2 * x + h) * 256 + y * HALF, HALF)
        own_b.append(keep(rhs.at[:, pl.ds(start, HALF), :], b8.at[y, :, pl.ds(h * HALF, HALF), :]))
    own_l = []
    for s in (1, 0):
        own_l.append(
            [keep(below.at[0, s], lf0.at[s, y, x]), keep(below.at[1, s], lf1.at[s, x, y])]
        )

    peers = [dict(dy=d) for d in range(1, NY)] + [dict(dx=d) for d in range(1, NX)]
    peers += [dict(dz=d) for d in range(1, NZ)] + [dict(dk=1)]
    barrier = pltpu.get_barrier_semaphore()
    for p in peers:
        pl.semaphore_signal(barrier, inc=1, device_id=at(**p), device_id_type=MESH)
    pl.semaphore_wait(barrier, len(peers))

    bcopies = []
    for d in (1, 3, 2):
        for h in range(2):
            start = pl.multiple_of((2 * x + h) * 256 + ((y + d) % NY) * HALF, HALF)
            bcopies.append(
                push(
                    rhs.at[:, pl.ds(start, HALF), :],
                    b8.at[y, :, pl.ds(h * HALF, HALF), :],
                    dy=d,
                )
            )

    def begin(a0, a1, own0, own1):
        hop = {}
        for d in (1, 3, 2):
            hop["x", d] = push(own0, a0.at[y, x], dx=d)
            hop["y", d] = push(own1, a1.at[x, y], dy=d)
        for d in (1, 3):
            hop["yy", d, 0] = push(own0, a0.at[y, x], dy=d)
            hop["xx", d, 0] = push(own1, a1.at[x, y], dx=d)
        return a0, a1, hop

    def forward(st):
        a0, a1, hop = st
        for e in (1, 3, 2):
            hop.pop(("x", e)).wait_recv()
            piece = a0.at[y, (x - e) % NX]
            for d in (1, 3):
                hop["yy", d, e] = push(piece, piece, dy=d)
            hop.pop(("y", e)).wait_recv()
            piece = a1.at[x, (y - e) % NY]
            for d in (1, 3):
                hop["xx", d, e] = push(piece, piece, dx=d)

    def relay(st):
        a0, a1, hop = st
        for i in range(2):
            for d, e in ((1, (0, 1)[i]), (3, (3, 2)[i])):
                hop.pop(("yy", d, e)).wait_recv()
                piece = a0.at[(y - d) % NY, (x - e) % NX]
                hop["far y", d, e] = push(piece, piece, dy=d)
                hop.pop(("xx", d, e)).wait_recv()
                piece = a1.at[(x - d) % NX, (y - e) % NY]
                hop["far x", d, e] = push(piece, piece, dx=d)

    def finish(st):
        for c in st[2].values():
            c.wait_recv()

    def arrive(cs):
        for c in cs:
            c.wait_recv()

    sd = begin(df0, df1, diag.at[0], diag.at[1])

    slots = [((i // 2) * NZ + z) * 2 + i % 2 for i in range(8)]

    def find(r, tiles):
        h = home[r]
        return tuple(jnp.where(h == slots[i], r, tiles[i]) for i in range(8))

    for c in ints:
        c.wait()
    tiles = lax.fori_loop(0, TILES, find, (jnp.int32(-1),) * 8, unroll=4)
    for s in range(SUPERS):
        used = counts[s]

        def hit(e, found):
            r = jnp.where(e < used, rows_ref[s, e], -2)
            return tuple(jnp.where(r == tiles[i], 1.0, found[i]) for i in range(8))

        found = lax.fori_loop(0, MAX_BELOW, hit, (jnp.float32(0.0),) * 8, unroll=4)
        for i in range(8):
            q = tiles[i] - s * TILES_SUP
            inside = (q >= 0) & (q < TILES_SUP)
            mask[(s * 10 + 8) * 8 + i] = jnp.where(inside, 1.0, 0.0)
            mask[(s * 10 + 9) * 8 + i] = found[i]
            for t in range(8):
                col_tile = 4 * (t // 2) + 2 * k + t % 2
                mask[(s * 10 + t) * 8 + i] = jnp.where(q == col_tile, 1.0, 0.0)

    forward(sd)
    for c in own_b:
        c.wait()
    arrive(bcopies)

    def place(s):
        def tile(t, carry):
            acc = jnp.zeros((ROWS, TILE), F32)
            for i in range(8):
                acc = acc + b8[i // 2, i % 2] * mask[(s * 10 + t) * 8 + i]
            part[s, t] = acc
            return carry

        lax.fori_loop(0, 8, tile, 0)

    def scatter(s):
        cs = []
        for d in (4, 3, 5, 2, 6, 1, 7):
            cs.append(push(part.at[s, (z + d) % NZ], rbuf.at[s, d - 1], dz=d))
        return cs

    def reduce(s):
        total = part[s, z]
        for d in range(1, NZ):
            total = total + rbuf[s, d - 1]
        chunk[s] = total
        res[s, z] = total

    def gather(s):
        cs = []
        for d in (4, 3, 5, 2, 6, 1, 7):
            cs.append(push(chunk.at[s], res.at[s, z], dz=d))
        return cs

    place(2)
    rs = scatter(2)
    relay(sd)
    s1 = begin(lf0.at[1], lf1.at[1], below.at[0, 1], below.at[1, 1])
    place(1)
    place(0)
    arrive(rs)
    reduce(2)
    ag = gather(2)
    forward(s1)
    for c in own:
        c.wait()
    finish(sd)

    def convert_d(i, carry):
        a, b = i // 4, i % 4
        rows = pl.ds(pl.multiple_of(b * 256, 256), 256)
        for j, v in ((0, df0[a, b]), (1, df1[b, a])):
            hi, lo = split(v)
            dhi[a, rows, j * TILE:(j + 1) * TILE] = hi
            dlo[a, rows, j * TILE:(j + 1) * TILE] = lo
        return carry

    def convert_l(s):
        def step(i, carry):
            a, b = i // 4, i % 4
            for j, v in ((0, lf0[s, a, b]), (1, lf1[s, b, a])):
                hi, lo = split(v)
                rows = pl.ds(pl.multiple_of(a * 256 + j * TILE, TILE), TILE)
                lhi[b, rows, :] = hi
                llo[b, rows, :] = lo
            return carry

        lax.fori_loop(0, 16, step, 0)

    def product(whi, wlo, n):
        a, b = xhi[...], xlo[...]
        w = whi[n]
        acc = jnp.dot(a, w, preferred_element_type=F32)
        acc = acc + jnp.dot(b, w, preferred_element_type=F32)
        return acc + jnp.dot(a, wlo[n], preferred_element_type=F32)

    def diag_step(s):
        for t in range(8):
            hi, lo = split(res[s, t])
            xhi[:, t * TILE:(t + 1) * TILE] = hi
            xlo[:, t * TILE:(t + 1) * TILE] = lo

        base = count[0]
        count[0] += 4

        def step(n, carry):
            spart[s, n] = product(dhi, dlo, n)
            trade(s, n, base).start()
            return carry

        lax.fori_loop(0, 4, step, 0)
        return base

    def trade(s, n, base):
        src, dst = (spart.at[s, n], exch.at[s, n]) if s else (spart.at[0, n, other, :], exch0.at[n])
        return pltpu.make_async_remote_copy(
            src_ref=src, dst_ref=dst, send_sem=send.at[base + n], recv_sem=recv.at[base + n],
            device_id=at(dk=1), device_id_type=MESH,
        )

    def lanes(s, row, n):
        lane = lax.broadcasted_iota(jnp.int32, (1, 256), 1)
        base = (s * 10 + row) * 8 + 2 * n
        return jnp.where(lane < TILE, mask[base], mask[base + 1])

    def absorb(s, target, ex):
        def step(n, carry):
            trade(s, n, ex).wait()
            v = jnp.where(lanes(s, 8, n) > 0.5, spart[s, n] + exch[s, n], 0.0)
            if s < SUPERS - 1:
                v = v + sol[n]
            sol[n] = v
            hi, lo = split(v * lanes(target, 9, n))
            where = pl.ds(pl.multiple_of(n * 256, 256), 256)
            xhi[:, where] = hi
            xlo[:, where] = lo
            return carry

        lax.fori_loop(0, 4, step, 0)

    def below_step(s):
        def step(n, carry):
            acc = product(lhi, llo, n)
            part[s, 2 * n] = part[s, 2 * n] - acc[:, :TILE]
            part[s, 2 * n + 1] = part[s, 2 * n + 1] - acc[:, TILE:]
            return carry

        lax.fori_loop(0, 4, step, 0)

    lax.fori_loop(0, 16, convert_d, 0)
    relay(s1)
    s0 = begin(lf0.at[0], lf1.at[0], below.at[0, 0], below.at[1, 0])
    arrive(ag)
    ex = diag_step(2)
    forward(s0)
    for c in own_l:
        for w in c:
            w.wait()
    finish(s1)
    convert_l(1)
    absorb(2, 1, ex)
    below_step(1)
    rs = scatter(1)
    relay(s0)
    arrive(rs)
    reduce(1)
    ag = gather(1)
    finish(s0)
    convert_l(0)
    arrive(ag)
    ex = diag_step(1)
    absorb(1, 0, ex)
    below_step(0)
    rs = scatter(0)
    arrive(rs)
    reduce(0)
    ag = gather(0)
    arrive(ag)
    ex = diag_step(0)
    for n in range(4):
        trade(0, n, ex).wait()
        v = spart[0, n, mine, :] + exch0[n]
        v = sol[n, mine, :] + jnp.where(lanes(0, 8, n) > 0.5, v, 0.0)
        outs[n, 0] = v[:, :TILE]
        outs[n, 1] = v[:, TILE:]
    oc = [push(outs.at[(y + d) % NY], outr.at[y], dy=d) for d in (1, 3, 2)]
    outr[y] = outs[y]
    arrive(oc)
    for n in range(4):
        for j in range(2):
            out[j, n * HALF:(n + 1) * HALF, :] = outr[n, j]
    for c in sent:
        c.wait_send()


COPIES = 180


def body(right_side, below_blocks, diag_cols, tile_home, block_rows, block_counts):
    vm = pltpu.VMEM
    hbm = pl.BlockSpec(memory_space=pltpu.HBM)
    return pl.pallas_call(
        kernel,
        name="solve",
        out_shape=jax.ShapeDtypeStruct((2, 256, TILE), F32),
        in_specs=[hbm] * 6,
        out_specs=pl.BlockSpec(memory_space=pltpu.VMEM),
        scratch_shapes=[
            pltpu.SMEM((TILES,), jnp.int32),
            pltpu.SMEM((SUPERS, MAX_BELOW), jnp.int32),
            pltpu.SMEM((SUPERS,), jnp.int32),
            pltpu.SMEM((SUPERS * 10 * 8,), F32),
            vm((4, 2, ROWS, TILE), F32),
            vm((4, 4, 256, TILE), F32),
            vm((4, 4, 256, TILE), F32),
            vm((2, 4, 4, TILE, 256), F32),
            vm((2, 4, 4, TILE, 256), F32),
            vm((4, 1024, 256), BF16),
            vm((4, 1024, 256), BF16),
            vm((4, 1024, 256), BF16),
            vm((4, 1024, 256), BF16),
            vm((ROWS, 1024), BF16),
            vm((ROWS, 1024), BF16),
            vm((3, 8, ROWS, TILE), F32),
            vm((3, 7, ROWS, TILE), F32),
            vm((3, ROWS, TILE), F32),
            vm((3, 8, ROWS, TILE), F32),
            vm((3, 4, ROWS, 256), F32),
            vm((3, 4, ROWS, 256), F32),
            vm((4, HALF, 256), F32),
            vm((4, ROWS, 256), F32),
            vm((4, 2, HALF, TILE), F32),
            vm((4, 2, HALF, TILE), F32),
            pltpu.SemaphoreType.DMA((COPIES,)),
            pltpu.SemaphoreType.DMA((COPIES,)),
            pltpu.SemaphoreType.DMA((12,)),
        ],
        compiler_params=pltpu.CompilerParams(
            collective_id=0, has_side_effects=True, vmem_limit_bytes=60 * 2**20
        ),
    )(tile_home, block_rows, block_counts, right_side, below_blocks, diag_cols)


def solution(mesh):
    return jax.shard_map(
        body,
        mesh=mesh,
        in_specs=(
            P("blk", None, None),
            P("blk", None, None, "col"),
            P("blk", "col", None),
            P(),
            P(),
            P(),
        ),
        out_specs=P("blk", "col", None),
        check_vma=False,
    )
```

```python
import jax
import jax.numpy as jnp
from jax import lax
from jax.experimental import pallas as pl
from jax.experimental.pallas import tpu as pltpu
from jax.sharding import PartitionSpec as P

TILE = 128
SUPERS = 3
SAMPLES = 2048
TILES_SUP = 16
TILES = 48
MAX_BELOW = 32
NX, NY, NZ = 4, 4, 8
ROWS = 128
HALF = 64
MESH = pl.DeviceIdType.MESH
F32 = jnp.float32
BF16 = jnp.bfloat16


def split(v):
    hi = v.astype(BF16)
    return hi, (v - hi.astype(F32)).astype(BF16)


def kernel(
    home_in, rows_in, counts_in, rhs, below, diag, out,
    home, rows_ref, counts, mask,
    b8, df0, df1, lf0, lf1, dhi, dlo, lhi, llo, xd, xl,
    part, rbuf, chunk, res, spart, exch, sol, outs, outr,
    send, recv, local,
):
    blk, col = lax.axis_index("blk"), lax.axis_index("col")
    y, z = blk // NZ, blk % NZ
    x, k = col // 2, col % 2
    count = [0, 0]

    def at(dy=0, dz=0, dx=0, dk=0):
        return (((y + dy) % NY) * NZ + (z + dz) % NZ, ((x + dx) % NX) * 2 + (k + dk) % 2)

    def push(src, dst, slot=None, **where):
        i = slot
        if slot is None:
            i = count[0]
            count[0] += 1
        c = pltpu.make_async_remote_copy(
            src_ref=src, dst_ref=dst, send_sem=send.at[i], recv_sem=recv.at[i],
            device_id=at(**where), device_id_type=MESH,
        )
        c.start()
        if slot is None:
            sent.append(c)
        return c

    def keep(src, dst):
        i = count[1]
        count[1] += 1
        c = pltpu.make_async_copy(src, dst, local.at[i])
        c.start()
        return c

    sent = []
    ints = [keep(home_in, home), keep(rows_in, rows_ref), keep(counts_in, counts)]
    own = [keep(diag.at[0], df0.at[y, x]), keep(diag.at[1], df1.at[x, y])]
    own_b = []
    for h in range(2):
        start = pl.multiple_of((2 * x + h) * 256 + y * HALF, HALF)
        own_b.append(keep(rhs.at[:, pl.ds(start, HALF), :], b8.at[y, :, pl.ds(h * HALF, HALF), :]))
    own_l = []
    for s in (1, 0):
        own_l.append(
            [keep(below.at[0, s], lf0.at[s, y, x]), keep(below.at[1, s], lf1.at[s, x, y])]
        )

    peers = [dict(dy=d) for d in range(1, NY)] + [dict(dx=d) for d in range(1, NX)]
    peers += [dict(dz=d) for d in range(1, NZ)] + [dict(dk=1)]
    barrier = pltpu.get_barrier_semaphore()
    for p in peers:
        pl.semaphore_signal(barrier, inc=1, device_id=at(**p), device_id_type=MESH)
    pl.semaphore_wait(barrier, len(peers))

    bcopies = []
    for d in (1, 3, 2):
        for h in range(2):
            start = pl.multiple_of((2 * x + h) * 256 + ((y + d) % NY) * HALF, HALF)
            bcopies.append(
                push(
                    rhs.at[:, pl.ds(start, HALF), :],
                    b8.at[y, :, pl.ds(h * HALF, HALF), :],
                    dy=d,
                )
            )

    def begin(a0, a1, own0, own1):
        hop = {}
        for d in (1, 3, 2):
            hop["x", d] = push(own0, a0.at[y, x], dx=d)
            hop["y", d] = push(own1, a1.at[x, y], dy=d)
        for d in (1, 3):
            hop["yy", d, 0] = push(own0, a0.at[y, x], dy=d)
            hop["xx", d, 0] = push(own1, a1.at[x, y], dx=d)
        return a0, a1, hop

    def forward(st):
        a0, a1, hop = st
        for e in (1, 3, 2):
            hop.pop(("x", e)).wait_recv()
            piece = a0.at[y, (x - e) % NX]
            for d in (1, 3):
                hop["yy", d, e] = push(piece, piece, dy=d)
            hop.pop(("y", e)).wait_recv()
            piece = a1.at[x, (y - e) % NY]
            for d in (1, 3):
                hop["xx", d, e] = push(piece, piece, dx=d)

    def relay(st):
        a0, a1, hop = st
        for i in range(2):
            for d, e in ((1, (0, 1)[i]), (3, (3, 2)[i])):
                hop.pop(("yy", d, e)).wait_recv()
                piece = a0.at[(y - d) % NY, (x - e) % NX]
                hop["far y", d, e] = push(piece, piece, dy=d)
                hop.pop(("xx", d, e)).wait_recv()
                piece = a1.at[(x - d) % NX, (y - e) % NY]
                hop["far x", d, e] = push(piece, piece, dx=d)

    def finish(st):
        for c in st[2].values():
            c.wait_recv()

    def arrive(cs):
        for c in cs:
            c.wait_recv()

    sd = begin(df0, df1, diag.at[0], diag.at[1])

    slots = [((i // 2) * NZ + z) * 2 + i % 2 for i in range(8)]

    def find(r, tiles):
        h = home[r]
        return tuple(jnp.where(h == slots[i], r, tiles[i]) for i in range(8))

    for c in ints:
        c.wait()
    tiles = lax.fori_loop(0, TILES, find, (jnp.int32(-1),) * 8, unroll=4)
    for s in range(SUPERS):
        used = counts[s]

        def hit(e, found):
            r = jnp.where(e < used, rows_ref[s, e], -2)
            return tuple(jnp.where(r == tiles[i], 1.0, found[i]) for i in range(8))

        found = lax.fori_loop(0, MAX_BELOW, hit, (jnp.float32(0.0),) * 8, unroll=4)
        for i in range(8):
            q = tiles[i] - s * TILES_SUP
            inside = (q >= 0) & (q < TILES_SUP)
            mask[(s * 10 + 8) * 8 + i] = jnp.where(inside, 1.0, 0.0)
            mask[(s * 10 + 9) * 8 + i] = found[i]
            for t in range(8):
                col_tile = 4 * (t // 2) + 2 * k + t % 2
                mask[(s * 10 + t) * 8 + i] = jnp.where(q == col_tile, 1.0, 0.0)

    forward(sd)
    for c in own_b:
        c.wait()
    arrive(bcopies)

    def place(s):
        def tile(t, carry):
            acc = jnp.zeros((ROWS, TILE), F32)
            for i in range(8):
                acc = acc + b8[i // 2, i % 2] * mask[(s * 10 + t) * 8 + i]
            part[s, 0, t] = acc[:HALF]
            part[s, 1, t] = acc[HALF:]
            return carry

        lax.fori_loop(0, 8, tile, 0)

    def scatter(s, h):
        cs = []
        for d in (4, 3, 5, 2, 6, 1, 7):
            cs.append(push(part.at[s, h, (z + d) % NZ], rbuf.at[s, h, d - 1], dz=d))
        return cs

    def turn(s, h, cs):
        arrive(cs)
        total = part[s, h, z]
        for d in range(1, NZ):
            total = total + rbuf[s, h, d - 1]
        chunk[s, h] = total
        res[s, h, z] = total
        return [push(chunk.at[s, h], res.at[s, h, z], dz=d) for d in (4, 3, 5, 2, 6, 1, 7)]

    place(2)
    rs = [scatter(2, 0), scatter(2, 1)]
    relay(sd)
    s1 = begin(lf0.at[1], lf1.at[1], below.at[0, 1], below.at[1, 1])
    place(1)
    place(0)
    ag = [turn(2, h, rs[h]) for h in range(2)]
    forward(s1)
    for c in own:
        c.wait()
    finish(sd)

    def convert_d(i, carry):
        a, b = i // 4, i % 4
        rows = pl.ds(pl.multiple_of(b * 256, 256), 256)
        for j, v in ((0, df0[a, b]), (1, df1[b, a])):
            hi, lo = split(v)
            dhi[a, rows, j * TILE:(j + 1) * TILE] = hi
            dlo[a, rows, j * TILE:(j + 1) * TILE] = lo
        return carry

    def convert_l(s):
        def step(i, carry):
            a, b = i // 4, i % 4
            for j, v in ((0, lf0[s, a, b]), (1, lf1[s, b, a])):
                hi, lo = split(v)
                rows = pl.ds(pl.multiple_of(a * 256 + j * TILE, TILE), TILE)
                lhi[b, rows, :] = hi
                llo[b, rows, :] = lo
            return carry

        lax.fori_loop(0, 16, step, 0)

    def product(xs, whi, wlo, n):
        both = jnp.dot(xs[...], whi[n], preferred_element_type=F32)
        cross = jnp.dot(xs[:HALF], wlo[n], preferred_element_type=F32)
        return both[:HALF] + (both[HALF:] + cross)

    def diag_step(s, h, cs):
        arrive(cs)
        for t in range(8):
            hi, lo = split(res[s, h, t])
            xd[:HALF, t * TILE:(t + 1) * TILE] = hi
            xd[HALF:, t * TILE:(t + 1) * TILE] = lo
        base = count[0]
        count[0] += 4

        def step(n, carry):
            spart[s, h, n] = product(xd, dhi, dlo, n)
            trade(s, h, n, base).start()
            return carry

        lax.fori_loop(0, 4, step, 0)
        return base

    def trade(s, h, n, base):
        return pltpu.make_async_remote_copy(
            src_ref=spart.at[s, h, n], dst_ref=exch.at[s, h, n],
            send_sem=send.at[base + n], recv_sem=recv.at[base + n],
            device_id=at(dk=1), device_id_type=MESH,
        )

    def lanes(s, row, n):
        lane = lax.broadcasted_iota(jnp.int32, (1, 256), 1)
        base = (s * 10 + row) * 8 + 2 * n
        return jnp.where(lane < TILE, mask[base], mask[base + 1])

    def below_step(s, h, ex):
        def weigh(n, carry):
            trade(s + 1, h, n, ex).wait()
            v = spart[s + 1, h, n] + exch[s + 1, h, n]
            v = jnp.where(lanes(s + 1, 8, n) > 0.5, v, 0.0)
            if s == 0:
                v = v + sol[h, n]
            sol[h, n] = v
            hi, lo = split(v * lanes(s, 9, n))
            where = pl.ds(pl.multiple_of(n * 256, 256), 256)
            xl[:HALF, where] = hi
            xl[HALF:, where] = lo
            return carry

        lax.fori_loop(0, 4, weigh, 0)

        def step(n, carry):
            acc = product(xl, lhi, llo, n)
            part[s, h, 2 * n] = part[s, h, 2 * n] - acc[:, :TILE]
            part[s, h, 2 * n + 1] = part[s, h, 2 * n + 1] - acc[:, TILE:]
            return carry

        lax.fori_loop(0, 4, step, 0)
        return scatter(s, h)

    lax.fori_loop(0, 16, convert_d, 0)
    relay(s1)
    s0 = begin(lf0.at[0], lf1.at[0], below.at[0, 0], below.at[1, 0])
    ex = [diag_step(2, h, ag[h]) for h in range(2)]
    forward(s0)
    for c in own_l:
        for w in c:
            w.wait()
    finish(s1)
    convert_l(1)
    rs = [below_step(1, h, ex[h]) for h in range(2)]
    relay(s0)
    ag = [turn(1, h, rs[h]) for h in range(2)]
    finish(s0)
    convert_l(0)
    ex0 = diag_step(1, 0, ag[0])
    rs0 = below_step(0, 0, ex0)
    ex1 = diag_step(1, 1, ag[1])
    rs1 = below_step(0, 1, ex1)
    ag = [turn(0, 0, rs0), turn(0, 1, rs1)]
    ex = [diag_step(0, h, ag[h]) for h in range(2)]
    for h in range(2):
        for n in range(4):
            trade(0, h, n, ex[h]).wait()
    for n in range(4):
        v = spart[0, k, n] + exch[0, k, n]
        v = sol[k, n] + jnp.where(lanes(0, 8, n) > 0.5, v, 0.0)
        outs[n, 0] = v[:, :TILE]
        outs[n, 1] = v[:, TILE:]
    oc = [push(outs.at[(y + d) % NY], outr.at[y], dy=d) for d in (1, 3, 2)]
    outr[y] = outs[y]
    arrive(oc)
    for n in range(4):
        for j in range(2):
            out[j, n * HALF:(n + 1) * HALF, :] = outr[n, j]
    for c in sent:
        c.wait_send()


COPIES = 240


def body(right_side, below_blocks, diag_cols, tile_home, block_rows, block_counts):
    vm = pltpu.VMEM
    hbm = pl.BlockSpec(memory_space=pltpu.HBM)
    return pl.pallas_call(
        kernel,
        name="solve",
        out_shape=jax.ShapeDtypeStruct((2, 256, TILE), F32),
        in_specs=[hbm] * 6,
        out_specs=pl.BlockSpec(memory_space=pltpu.VMEM),
        scratch_shapes=[
            pltpu.SMEM((TILES,), jnp.int32),
            pltpu.SMEM((SUPERS, MAX_BELOW), jnp.int32),
            pltpu.SMEM((SUPERS,), jnp.int32),
            pltpu.SMEM((SUPERS * 10 * 8,), F32),
            vm((4, 2, ROWS, TILE), F32),
            vm((4, 4, 256, TILE), F32),
            vm((4, 4, 256, TILE), F32),
            vm((2, 4, 4, TILE, 256), F32),
            vm((2, 4, 4, TILE, 256), F32),
            vm((4, 1024, 256), BF16),
            vm((4, 1024, 256), BF16),
            vm((4, 1024, 256), BF16),
            vm((4, 1024, 256), BF16),
            vm((ROWS, 1024), BF16),
            vm((ROWS, 1024), BF16),
            vm((3, 2, 8, HALF, TILE), F32),
            vm((3, 2, 7, HALF, TILE), F32),
            vm((3, 2, HALF, TILE), F32),
            vm((3, 2, 8, HALF, TILE), F32),
            vm((3, 2, 4, HALF, 256), F32),
            vm((3, 2, 4, HALF, 256), F32),
            vm((2, 4, HALF, 256), F32),
            vm((4, 2, HALF, TILE), F32),
            vm((4, 2, HALF, TILE), F32),
            pltpu.SemaphoreType.DMA((COPIES,)),
            pltpu.SemaphoreType.DMA((COPIES,)),
            pltpu.SemaphoreType.DMA((12,)),
        ],
        compiler_params=pltpu.CompilerParams(
            collective_id=0, has_side_effects=True, vmem_limit_bytes=60 * 2**20
        ),
    )(tile_home, block_rows, block_counts, right_side, below_blocks, diag_cols)


def solution(mesh):
    return jax.shard_map(
        body,
        mesh=mesh,
        in_specs=(
            P("blk", None, None),
            P("blk", None, None, "col"),
            P("blk", "col", None),
            P(),
            P(),
            P(),
        ),
        out_specs=P("blk", "col", None),
        check_vma=False,
    )
```

```python
import jax
import jax.numpy as jnp
from jax import lax
from jax.experimental import pallas as pl
from jax.experimental.pallas import tpu as pltpu
from jax.sharding import PartitionSpec as P

TILE = 128
SUPERS = 3
SAMPLES = 2048
TILES_SUP = 16
TILES = 48
MAX_BELOW = 32
NX, NY, NZ = 4, 4, 8
ROWS = 128
HALF = 64
MESH = pl.DeviceIdType.MESH
F32 = jnp.float32
BF16 = jnp.bfloat16


def split(v):
    hi = v.astype(BF16)
    return hi, (v - hi.astype(F32)).astype(BF16)


def kernel(
    home_in, rows_in, counts_in, rhs, below, diag, out,
    home, rows_ref, counts, mask,
    b8, df0, df1, lf0, lf1, dhi, dlo, lhi, llo, xd, xl,
    part, rbuf, chunk, res, spart, exch, sol, outs, outr,
    send, recv, local,
):
    blk, col = lax.axis_index("blk"), lax.axis_index("col")
    y, z = blk // NZ, blk % NZ
    x, k = col // 2, col % 2
    count = [0, 0]

    def at(dy=0, dz=0, dx=0, dk=0):
        return (((y + dy) % NY) * NZ + (z + dz) % NZ, ((x + dx) % NX) * 2 + (k + dk) % 2)

    def push(src, dst, slot=None, **where):
        i = slot
        if slot is None:
            i = count[0]
            count[0] += 1
        c = pltpu.make_async_remote_copy(
            src_ref=src, dst_ref=dst, send_sem=send.at[i], recv_sem=recv.at[i],
            device_id=at(**where), device_id_type=MESH,
        )
        c.start()
        if slot is None:
            sent.append(c)
        return c

    def keep(src, dst):
        i = count[1]
        count[1] += 1
        c = pltpu.make_async_copy(src, dst, local.at[i])
        c.start()
        return c

    sent = []
    ints = [keep(home_in, home), keep(rows_in, rows_ref), keep(counts_in, counts)]
    own = [keep(diag.at[0], df0.at[y, x]), keep(diag.at[1], df1.at[x, y])]
    own_b = []
    for h in range(2):
        start = pl.multiple_of((2 * x + h) * 256 + y * HALF, HALF)
        own_b.append(keep(rhs.at[:, pl.ds(start, HALF), :], b8.at[y, :, pl.ds(h * HALF, HALF), :]))
    own_l = []
    for s in (1, 0):
        own_l.append(
            [keep(below.at[0, s], lf0.at[s, y, x]), keep(below.at[1, s], lf1.at[s, x, y])]
        )

    peers = [dict(dy=d) for d in range(1, NY)] + [dict(dx=d) for d in range(1, NX)]
    peers += [dict(dz=d) for d in range(1, NZ)] + [dict(dk=1)]
    barrier = pltpu.get_barrier_semaphore()
    for p in peers:
        pl.semaphore_signal(barrier, inc=1, device_id=at(**p), device_id_type=MESH)
    pl.semaphore_wait(barrier, len(peers))

    bcopies = []
    for d in (1, 3, 2):
        for h in range(2):
            start = pl.multiple_of((2 * x + h) * 256 + ((y + d) % NY) * HALF, HALF)
            bcopies.append(
                push(
                    rhs.at[:, pl.ds(start, HALF), :],
                    b8.at[y, :, pl.ds(h * HALF, HALF), :],
                    dy=d,
                )
            )

    def begin(a0, a1, own0, own1):
        hop = {}
        for d in (1, 3, 2):
            hop["x", d] = push(own0, a0.at[y, x], dx=d)
            hop["y", d] = push(own1, a1.at[x, y], dy=d)
        for d in (1, 3):
            hop["yy", d, 0] = push(own0, a0.at[y, x], dy=d)
            hop["xx", d, 0] = push(own1, a1.at[x, y], dx=d)
        return a0, a1, hop

    def forward(st):
        a0, a1, hop = st
        for e in (1, 3, 2):
            hop.pop(("x", e)).wait_recv()
            piece = a0.at[y, (x - e) % NX]
            for d in (1, 3):
                hop["yy", d, e] = push(piece, piece, dy=d)
            hop.pop(("y", e)).wait_recv()
            piece = a1.at[x, (y - e) % NY]
            for d in (1, 3):
                hop["xx", d, e] = push(piece, piece, dx=d)

    def relay(st):
        a0, a1, hop = st
        for i in range(2):
            for d, e in ((1, (0, 1)[i]), (3, (3, 2)[i])):
                hop.pop(("yy", d, e)).wait_recv()
                piece = a0.at[(y - d) % NY, (x - e) % NX]
                hop["far y", d, e] = push(piece, piece, dy=d)
                hop.pop(("xx", d, e)).wait_recv()
                piece = a1.at[(x - d) % NX, (y - e) % NY]
                hop["far x", d, e] = push(piece, piece, dx=d)

    def finish(st):
        for c in st[2].values():
            c.wait_recv()

    def arrive(cs):
        for c in cs:
            c.wait_recv()

    sd = begin(df0, df1, diag.at[0], diag.at[1])

    slots = [((i // 2) * NZ + z) * 2 + i % 2 for i in range(8)]

    def find(r, tiles):
        h = home[r]
        return tuple(jnp.where(h == slots[i], r, tiles[i]) for i in range(8))

    for c in ints:
        c.wait()
    tiles = lax.fori_loop(0, TILES, find, (jnp.int32(-1),) * 8, unroll=4)
    for s in range(SUPERS):
        used = counts[s]

        def hit(e, found):
            r = jnp.where(e < used, rows_ref[s, e], -2)
            return tuple(jnp.where(r == tiles[i], 1.0, found[i]) for i in range(8))

        found = lax.fori_loop(0, MAX_BELOW, hit, (jnp.float32(0.0),) * 8, unroll=4)
        for i in range(8):
            q = tiles[i] - s * TILES_SUP
            inside = (q >= 0) & (q < TILES_SUP)
            mask[(s * 10 + 8) * 8 + i] = jnp.where(inside, 1.0, 0.0)
            mask[(s * 10 + 9) * 8 + i] = found[i]
            for t in range(8):
                col_tile = 4 * (t // 2) + 2 * k + t % 2
                mask[(s * 10 + t) * 8 + i] = jnp.where(q == col_tile, 1.0, 0.0)

    forward(sd)
    for c in own_b:
        c.wait()
    arrive(bcopies)

    def place(s):
        def tile(t, carry):
            acc = jnp.zeros((ROWS, TILE), F32)
            for i in range(8):
                acc = acc + b8[i // 2, i % 2] * mask[(s * 10 + t) * 8 + i]
            part[s, 0, t] = acc[:HALF]
            part[s, 1, t] = acc[HALF:]
            return carry

        lax.fori_loop(0, 8, tile, 0)

    def scatter(s, h):
        cs = []
        for d in (4, 3, 5, 2, 6, 1, 7):
            cs.append(push(part.at[s, h, (z + d) % NZ], rbuf.at[s, h, d - 1], dz=d))
        return cs

    def turn(s, h, cs):
        arrive(cs)
        total = part[s, h, z]
        for d in range(1, NZ):
            total = total + rbuf[s, h, d - 1]
        chunk[s, h] = total
        res[s, h, z] = total
        return [push(chunk.at[s, h], res.at[s, h, z], dz=d) for d in (4, 3, 5, 2, 6, 1, 7)]

    place(2)
    rs = [scatter(2, 0), scatter(2, 1)]
    relay(sd)
    s1 = begin(lf0.at[1], lf1.at[1], below.at[0, 1], below.at[1, 1])
    place(1)
    place(0)
    ag = [turn(2, h, rs[h]) for h in range(2)]
    forward(s1)
    for c in own:
        c.wait()
    finish(sd)

    def convert_d(i, carry):
        a, b = i // 4, i % 4
        rows = pl.ds(pl.multiple_of(b * 256, 256), 256)
        for j, v in ((0, df0[a, b]), (1, df1[b, a])):
            hi, lo = split(v)
            dhi[a, rows, j * TILE:(j + 1) * TILE] = hi
            dlo[a, rows, j * TILE:(j + 1) * TILE] = lo
        return carry

    def convert_l(s):
        def step(i, carry):
            a, b = i // 4, i % 4
            for j, v in ((0, lf0[s, a, b]), (1, lf1[s, b, a])):
                hi, lo = split(v)
                rows = pl.ds(pl.multiple_of(a * 256 + j * TILE, TILE), TILE)
                lhi[b, rows, :] = hi
                llo[b, rows, :] = lo
            return carry

        lax.fori_loop(0, 16, step, 0)

    def product(xs, whi, wlo, n):
        both = jnp.dot(xs[...], whi[n], preferred_element_type=F32)
        cross = jnp.dot(xs[:HALF], wlo[n], preferred_element_type=F32)
        return both[:HALF] + (both[HALF:] + cross)

    def diag_step(s, h, cs):
        arrive(cs)
        for t in range(8):
            hi, lo = split(res[s, h, t])
            xd[:HALF, t * TILE:(t + 1) * TILE] = hi
            xd[HALF:, t * TILE:(t + 1) * TILE] = lo
        base = count[0]
        count[0] += 4

        def step(n, carry):
            spart[s, h, n] = product(xd, dhi, dlo, n)
            trade(s, h, n, base).start()
            return carry

        lax.fori_loop(0, 4, step, 0)
        return base

    def trade(s, h, n, base):
        return pltpu.make_async_remote_copy(
            src_ref=spart.at[s, h, n], dst_ref=exch.at[s, h, n],
            send_sem=send.at[base + n], recv_sem=recv.at[base + n],
            device_id=at(dk=1), device_id_type=MESH,
        )

    def lanes(s, row, n):
        lane = lax.broadcasted_iota(jnp.int32, (1, 256), 1)
        base = (s * 10 + row) * 8 + 2 * n
        return jnp.where(lane < TILE, mask[base], mask[base + 1])

    def below_step(s, h, ex):
        def weigh(n, carry):
            trade(s + 1, h, n, ex).wait()
            v = spart[s + 1, h, n] + exch[s + 1, h, n]
            v = jnp.where(lanes(s + 1, 8, n) > 0.5, v, 0.0)
            if s == 0:
                v = v + sol[h, n]
            sol[h, n] = v
            hi, lo = split(v * lanes(s, 9, n))
            where = pl.ds(pl.multiple_of(n * 256, 256), 256)
            xl[:HALF, where] = hi
            xl[HALF:, where] = lo
            return carry

        lax.fori_loop(0, 4, weigh, 0)

        def step(n, carry):
            acc = product(xl, lhi, llo, n)
            part[s, h, 2 * n] = part[s, h, 2 * n] - acc[:, :TILE]
            part[s, h, 2 * n + 1] = part[s, h, 2 * n + 1] - acc[:, TILE:]
            return carry

        lax.fori_loop(0, 4, step, 0)
        return scatter(s, h)

    lax.fori_loop(0, 16, convert_d, 0)
    relay(s1)
    ex = [diag_step(2, h, ag[h]) for h in range(2)]
    s0 = begin(lf0.at[0], lf1.at[0], below.at[0, 0], below.at[1, 0])
    for c in own_l:
        for w in c:
            w.wait()
    finish(s1)
    convert_l(1)
    rs = [below_step(1, h, ex[h]) for h in range(2)]
    forward(s0)
    ag = [turn(1, h, rs[h]) for h in range(2)]
    relay(s0)
    ex0 = diag_step(1, 0, ag[0])
    finish(s0)
    convert_l(0)
    rs0 = below_step(0, 0, ex0)
    ex1 = diag_step(1, 1, ag[1])
    rs1 = below_step(0, 1, ex1)
    ag = [turn(0, 0, rs0), turn(0, 1, rs1)]
    ex = [diag_step(0, h, ag[h]) for h in range(2)]
    for h in range(2):
        for n in range(4):
            trade(0, h, n, ex[h]).wait()
    for n in range(4):
        v = spart[0, k, n] + exch[0, k, n]
        v = sol[k, n] + jnp.where(lanes(0, 8, n) > 0.5, v, 0.0)
        outs[n, 0] = v[:, :TILE]
        outs[n, 1] = v[:, TILE:]
    oc = [push(outs.at[(y + d) % NY], outr.at[y], dy=d) for d in (1, 3, 2)]
    outr[y] = outs[y]
    arrive(oc)
    for n in range(4):
        for j in range(2):
            out[j, n * HALF:(n + 1) * HALF, :] = outr[n, j]
    for c in sent:
        c.wait_send()


COPIES = 240


def body(right_side, below_blocks, diag_cols, tile_home, block_rows, block_counts):
    vm = pltpu.VMEM
    hbm = pl.BlockSpec(memory_space=pltpu.HBM)
    return pl.pallas_call(
        kernel,
        name="solve",
        out_shape=jax.ShapeDtypeStruct((2, 256, TILE), F32),
        in_specs=[hbm] * 6,
        out_specs=pl.BlockSpec(memory_space=pltpu.VMEM),
        scratch_shapes=[
            pltpu.SMEM((TILES,), jnp.int32),
            pltpu.SMEM((SUPERS, MAX_BELOW), jnp.int32),
            pltpu.SMEM((SUPERS,), jnp.int32),
            pltpu.SMEM((SUPERS * 10 * 8,), F32),
            vm((4, 2, ROWS, TILE), F32),
            vm((4, 4, 256, TILE), F32),
            vm((4, 4, 256, TILE), F32),
            vm((2, 4, 4, TILE, 256), F32),
            vm((2, 4, 4, TILE, 256), F32),
            vm((4, 1024, 256), BF16),
            vm((4, 1024, 256), BF16),
            vm((4, 1024, 256), BF16),
            vm((4, 1024, 256), BF16),
            vm((ROWS, 1024), BF16),
            vm((ROWS, 1024), BF16),
            vm((3, 2, 8, HALF, TILE), F32),
            vm((3, 2, 7, HALF, TILE), F32),
            vm((3, 2, HALF, TILE), F32),
            vm((3, 2, 8, HALF, TILE), F32),
            vm((3, 2, 4, HALF, 256), F32),
            vm((3, 2, 4, HALF, 256), F32),
            vm((2, 4, HALF, 256), F32),
            vm((4, 2, HALF, TILE), F32),
            vm((4, 2, HALF, TILE), F32),
            pltpu.SemaphoreType.DMA((COPIES,)),
            pltpu.SemaphoreType.DMA((COPIES,)),
            pltpu.SemaphoreType.DMA((12,)),
        ],
        compiler_params=pltpu.CompilerParams(
            collective_id=0, has_side_effects=True, vmem_limit_bytes=60 * 2**20
        ),
    )(tile_home, block_rows, block_counts, right_side, below_blocks, diag_cols)


def solution(mesh):
    return jax.shard_map(
        body,
        mesh=mesh,
        in_specs=(
            P("blk", None, None),
            P("blk", None, None, "col"),
            P("blk", "col", None),
            P(),
            P(),
            P(),
        ),
        out_specs=P("blk", "col", None),
        check_vma=False,
    )
```

```python
import jax
import jax.numpy as jnp
from jax import lax
from jax.experimental import pallas as pl
from jax.experimental.pallas import tpu as pltpu
from jax.sharding import PartitionSpec as P

TILE = 128
SUPERS = 3
SAMPLES = 2048
TILES_SUP = 16
TILES = 48
MAX_BELOW = 32
NX, NY, NZ = 4, 4, 8
ROWS = 128
HALF = 64
MESH = pl.DeviceIdType.MESH
F32 = jnp.float32
BF16 = jnp.bfloat16


def split(v):
    hi = v.astype(BF16)
    return hi, (v - hi.astype(F32)).astype(BF16)


def kernel(
    home_in, rows_in, counts_in, rhs, below, diag, out,
    home, rows_ref, counts, mask,
    b8, df0, df1, lf0, lf1, dhi, dlo, lhi, llo, xd, xl,
    part, rbuf, chunk, res, spart, exch, sol, outs, outr,
    send, recv, local,
):
    blk, col = lax.axis_index("blk"), lax.axis_index("col")
    y, z = blk // NZ, blk % NZ
    x, k = col // 2, col % 2
    count = [0, 0]

    def at(dy=0, dz=0, dx=0, dk=0):
        return (((y + dy) % NY) * NZ + (z + dz) % NZ, ((x + dx) % NX) * 2 + (k + dk) % 2)

    def push(src, dst, slot=None, **where):
        i = slot
        if slot is None:
            i = count[0]
            count[0] += 1
        c = pltpu.make_async_remote_copy(
            src_ref=src, dst_ref=dst, send_sem=send.at[i], recv_sem=recv.at[i],
            device_id=at(**where), device_id_type=MESH,
        )
        c.start()
        if slot is None:
            sent.append(c)
        return c

    def keep(src, dst):
        i = count[1]
        count[1] += 1
        c = pltpu.make_async_copy(src, dst, local.at[i])
        c.start()
        return c

    sent = []
    ints = [keep(home_in, home), keep(rows_in, rows_ref), keep(counts_in, counts)]
    own = [keep(diag.at[0], df0.at[y, x]), keep(diag.at[1], df1.at[x, y])]
    own_b = []
    for h in range(2):
        start = pl.multiple_of((2 * x + h) * 256 + y * HALF, HALF)
        own_b.append(keep(rhs.at[:, pl.ds(start, HALF), :], b8.at[y, :, pl.ds(h * HALF, HALF), :]))
    own_l = []
    for s in (1, 0):
        own_l.append(
            [keep(below.at[0, s], lf0.at[s, y, x]), keep(below.at[1, s], lf1.at[s, x, y])]
        )

    peers = [dict(dy=d) for d in range(1, NY)] + [dict(dx=d) for d in range(1, NX)]
    peers += [dict(dz=d) for d in range(1, NZ)] + [dict(dk=1)] + [dict(dy=d, dk=1) for d in range(1, NY)]
    barrier = pltpu.get_barrier_semaphore()
    for p in peers:
        pl.semaphore_signal(barrier, inc=1, device_id=at(**p), device_id_type=MESH)
    pl.semaphore_wait(barrier, len(peers))

    half = pl.ds(pl.multiple_of(k * HALF, HALF), HALF)
    bcopies = []
    for d in (1, 3, 2):
        start = pl.multiple_of((2 * x + k) * 256 + ((y + d) % NY) * HALF, HALF)
        bcopies.append(push(rhs.at[:, pl.ds(start, HALF), :], b8.at[y, :, half, :], dy=d))

    def begin(a0, a1, own0, own1):
        hop = {}
        for d in (1, 3, 2):
            hop["x", d] = push(own0, a0.at[y, x], dx=d)
            hop["y", d] = push(own1, a1.at[x, y], dy=d)
        for d in (1, 3):
            hop["yy", d, 0] = push(own0, a0.at[y, x], dy=d)
            hop["xx", d, 0] = push(own1, a1.at[x, y], dx=d)
        return a0, a1, hop

    def forward(st):
        a0, a1, hop = st
        for e in (1, 3, 2):
            hop.pop(("x", e)).wait_recv()
            piece = a0.at[y, (x - e) % NX]
            for d in (1, 3):
                hop["yy", d, e] = push(piece, piece, dy=d)
            hop.pop(("y", e)).wait_recv()
            piece = a1.at[x, (y - e) % NY]
            for d in (1, 3):
                hop["xx", d, e] = push(piece, piece, dx=d)

    def relay(st):
        a0, a1, hop = st
        for i in range(2):
            for d, e in ((1, (0, 1)[i]), (3, (3, 2)[i])):
                hop.pop(("yy", d, e)).wait_recv()
                piece = a0.at[(y - d) % NY, (x - e) % NX]
                hop["far y", d, e] = push(piece, piece, dy=d)
                hop.pop(("xx", d, e)).wait_recv()
                piece = a1.at[(x - d) % NX, (y - e) % NY]
                hop["far x", d, e] = push(piece, piece, dx=d)

    def finish(st):
        for c in st[2].values():
            c.wait_recv()

    def arrive(cs):
        for c in cs:
            c.wait_recv()

    sd = begin(df0, df1, diag.at[0], diag.at[1])

    slots = [((i // 2) * NZ + z) * 2 + i % 2 for i in range(8)]

    def find(r, tiles):
        h = home[r]
        return tuple(jnp.where(h == slots[i], r, tiles[i]) for i in range(8))

    for c in ints:
        c.wait()
    tiles = lax.fori_loop(0, TILES, find, (jnp.int32(-1),) * 8, unroll=4)
    for s in range(SUPERS):
        used = counts[s]

        def hit(e, found):
            r = jnp.where(e < used, rows_ref[s, e], -2)
            return tuple(jnp.where(r == tiles[i], 1.0, found[i]) for i in range(8))

        found = lax.fori_loop(0, MAX_BELOW, hit, (jnp.float32(0.0),) * 8, unroll=4)
        for i in range(8):
            q = tiles[i] - s * TILES_SUP
            inside = (q >= 0) & (q < TILES_SUP)
            mask[(s * 10 + 8) * 8 + i] = jnp.where(inside, 1.0, 0.0)
            mask[(s * 10 + 9) * 8 + i] = found[i]
            for t in range(8):
                col_tile = 4 * (t // 2) + 2 * k + t % 2
                mask[(s * 10 + t) * 8 + i] = jnp.where(q == col_tile, 1.0, 0.0)

    forward(sd)
    for c in own_b:
        c.wait()
    swaps = []
    for d, c in zip((1, 3, 2), bcopies):
        c.wait_recv()
        piece = b8.at[(y - d) % NY, :, half, :]
        swaps.append(push(piece, piece, dk=1))
    arrive(swaps)

    def place(s):
        def tile(t, carry):
            acc = jnp.zeros((ROWS, TILE), F32)
            for i in range(8):
                acc = acc + b8[i // 2, i % 2] * mask[(s * 10 + t) * 8 + i]
            part[s, 0, t] = acc[:HALF]
            part[s, 1, t] = acc[HALF:]
            return carry

        lax.fori_loop(0, 8, tile, 0)

    def scatter(s, h):
        cs = []
        for d in (4, 3, 5, 2, 6, 1, 7):
            cs.append(push(part.at[s, h, (z + d) % NZ], rbuf.at[s, h, d - 1], dz=d))
        return cs

    def turn(s, h, cs):
        arrive(cs)
        total = part[s, h, z]
        for d in range(1, NZ):
            total = total + rbuf[s, h, d - 1]
        chunk[s, h] = total
        res[s, h, z] = total
        return [push(chunk.at[s, h], res.at[s, h, z], dz=d) for d in (4, 3, 5, 2, 6, 1, 7)]

    place(2)
    rs = [scatter(2, 0), scatter(2, 1)]
    relay(sd)
    s1 = begin(lf0.at[1], lf1.at[1], below.at[0, 1], below.at[1, 1])
    place(1)
    place(0)
    ag = [turn(2, h, rs[h]) for h in range(2)]
    forward(s1)
    for c in own:
        c.wait()
    finish(sd)

    def convert_d(i, carry):
        a, b = i // 4, i % 4
        rows = pl.ds(pl.multiple_of(b * 256, 256), 256)
        for j, v in ((0, df0[a, b]), (1, df1[b, a])):
            hi, lo = split(v)
            dhi[a, rows, j * TILE:(j + 1) * TILE] = hi
            dlo[a, rows, j * TILE:(j + 1) * TILE] = lo
        return carry

    def convert_l(s):
        def step(i, carry):
            a, b = i // 4, i % 4
            for j, v in ((0, lf0[s, a, b]), (1, lf1[s, b, a])):
                hi, lo = split(v)
                rows = pl.ds(pl.multiple_of(a * 256 + j * TILE, TILE), TILE)
                lhi[b, rows, :] = hi
                llo[b, rows, :] = lo
            return carry

        lax.fori_loop(0, 16, step, 0)

    def product(xs, whi, wlo, n):
        both = jnp.dot(xs[...], whi[n], preferred_element_type=F32)
        cross = jnp.dot(xs[:HALF], wlo[n], preferred_element_type=F32)
        return both[:HALF] + (both[HALF:] + cross)

    def fill(s, h, cs):
        arrive(cs)
        for t in range(8):
            hi, lo = split(res[s, h, t])
            xd[:HALF, t * TILE:(t + 1) * TILE] = hi
            xd[HALF:, t * TILE:(t + 1) * TILE] = lo

    def diag_step(s, h, cs):
        fill(s, h, cs)
        base = count[0]
        count[0] += 4

        def step(n, carry):
            spart[s, h, n] = product(xd, dhi, dlo, n)
            trade(s, h, n, base).start()
            return carry

        lax.fori_loop(0, 4, step, 0)
        return base

    def trade(s, h, n, base):
        return pltpu.make_async_remote_copy(
            src_ref=spart.at[s, h, n], dst_ref=exch.at[s, h, n],
            send_sem=send.at[base + n], recv_sem=recv.at[base + n],
            device_id=at(dk=1), device_id_type=MESH,
        )

    def lanes(s, row, n):
        lane = lax.broadcasted_iota(jnp.int32, (1, 256), 1)
        base = (s * 10 + row) * 8 + 2 * n
        return jnp.where(lane < TILE, mask[base], mask[base + 1])

    def below_step(s, h, ex):
        def weigh(n, carry):
            trade(s + 1, h, n, ex).wait()
            v = spart[s + 1, h, n] + exch[s + 1, h, n]
            v = jnp.where(lanes(s + 1, 8, n) > 0.5, v, 0.0)
            if s == 0:
                v = v + sol[h, n]
            sol[h, n] = v
            hi, lo = split(v * lanes(s, 9, n))
            where = pl.ds(pl.multiple_of(n * 256, 256), 256)
            xl[:HALF, where] = hi
            xl[HALF:, where] = lo
            return carry

        lax.fori_loop(0, 4, weigh, 0)

        def step(n, carry):
            acc = product(xl, lhi, llo, n)
            part[s, h, 2 * n] = part[s, h, 2 * n] - acc[:, :TILE]
            part[s, h, 2 * n + 1] = part[s, h, 2 * n + 1] - acc[:, TILE:]
            return carry

        lax.fori_loop(0, 4, step, 0)
        return scatter(s, h)

    lax.fori_loop(0, 16, convert_d, 0)
    relay(s1)
    ex = [diag_step(2, h, ag[h]) for h in range(2)]
    s0 = begin(lf0.at[0], lf1.at[0], below.at[0, 0], below.at[1, 0])
    for c in own_l:
        for w in c:
            w.wait()
    finish(s1)
    convert_l(1)
    rs = [below_step(1, h, ex[h]) for h in range(2)]
    forward(s0)
    ag = [turn(1, h, rs[h]) for h in range(2)]
    relay(s0)
    ex0 = diag_step(1, 0, ag[0])
    finish(s0)
    convert_l(0)
    rs0 = below_step(0, 0, ex0)
    ex1 = diag_step(1, 1, ag[1])
    rs1 = below_step(0, 1, ex1)
    ag = [turn(0, 0, rs0), turn(0, 1, rs1)]
    base = count[0]
    count[0] += 16

    def last(h, d):
        rel = (h + k) % 2
        return pltpu.make_async_remote_copy(
            src_ref=outs.at[h, (y + d) % NY], dst_ref=outr.at[rel, y],
            send_sem=send.at[base + 4 * h + d], recv_sem=recv.at[base + 8 + 4 * rel + d],
            device_id=(((y + d) % NY) * NZ + z, x * 2 + h), device_id_type=MESH,
        )

    def landed(rel, d):
        return pltpu.make_async_remote_copy(
            src_ref=outs.at[0, y], dst_ref=outr.at[rel, (y - d) % NY],
            send_sem=send.at[base + 8 + 4 * rel + d], recv_sem=recv.at[base + 8 + 4 * rel + d],
            device_id=at(dy=d, dk=rel), device_id_type=MESH,
        )

    for h in range(2):
        fill(0, h, ag[h])

        def closing(n, carry):
            v = jnp.where(lanes(0, 8, n) > 0.5, product(xd, dhi, dlo, n), 0.0)
            mine = jnp.full((1, 256), jnp.where(k == h, 1.0, 0.0), F32) > 0.5
            outs[h, n] = v + jnp.where(mine, sol[h, n], 0.0)
            return carry

        lax.fori_loop(0, 4, closing, 0)
        for d in (1, 3, 2):
            last(h, d).start()

        @pl.when(k != h)
        def _():
            last(h, 0).start()

    outr[0, y] = outs[k, y]
    for rel in range(2):
        for d in (1, 3, 2, 0):
            if rel or d:
                landed(rel, d).wait_recv()
    for n in range(4):
        v = outr[0, n] + outr[1, n]
        for j in range(2):
            out[j, n * HALF:(n + 1) * HALF, :] = v[:, j * TILE:(j + 1) * TILE]
    for h in range(2):
        for d in (1, 3, 2):
            last(h, d).wait_send()

        @pl.when(k != h)
        def _():
            last(h, 0).wait_send()

    for c in sent:
        c.wait_send()


COPIES = 240


def body(right_side, below_blocks, diag_cols, tile_home, block_rows, block_counts):
    vm = pltpu.VMEM
    hbm = pl.BlockSpec(memory_space=pltpu.HBM)
    return pl.pallas_call(
        kernel,
        name="solve",
        out_shape=jax.ShapeDtypeStruct((2, 256, TILE), F32),
        in_specs=[hbm] * 6,
        out_specs=pl.BlockSpec(memory_space=pltpu.VMEM),
        scratch_shapes=[
            pltpu.SMEM((TILES,), jnp.int32),
            pltpu.SMEM((SUPERS, MAX_BELOW), jnp.int32),
            pltpu.SMEM((SUPERS,), jnp.int32),
            pltpu.SMEM((SUPERS * 10 * 8,), F32),
            vm((4, 2, ROWS, TILE), F32),
            vm((4, 4, 256, TILE), F32),
            vm((4, 4, 256, TILE), F32),
            vm((2, 4, 4, TILE, 256), F32),
            vm((2, 4, 4, TILE, 256), F32),
            vm((4, 1024, 256), BF16),
            vm((4, 1024, 256), BF16),
            vm((4, 1024, 256), BF16),
            vm((4, 1024, 256), BF16),
            vm((ROWS, 1024), BF16),
            vm((ROWS, 1024), BF16),
            vm((3, 2, 8, HALF, TILE), F32),
            vm((3, 2, 7, HALF, TILE), F32),
            vm((3, 2, HALF, TILE), F32),
            vm((3, 2, 8, HALF, TILE), F32),
            vm((3, 2, 4, HALF, 256), F32),
            vm((3, 2, 4, HALF, 256), F32),
            vm((2, 4, HALF, 256), F32),
            vm((2, 4, HALF, 256), F32),
            vm((2, 4, HALF, 256), F32),
            pltpu.SemaphoreType.DMA((COPIES,)),
            pltpu.SemaphoreType.DMA((COPIES,)),
            pltpu.SemaphoreType.DMA((12,)),
        ],
        compiler_params=pltpu.CompilerParams(
            collective_id=0, has_side_effects=True, vmem_limit_bytes=60 * 2**20
        ),
    )(tile_home, block_rows, block_counts, right_side, below_blocks, diag_cols)


def solution(mesh):
    return jax.shard_map(
        body,
        mesh=mesh,
        in_specs=(
            P("blk", None, None),
            P("blk", None, None, "col"),
            P("blk", "col", None),
            P(),
            P(),
            P(),
        ),
        out_specs=P("blk", "col", None),
        check_vma=False,
    )
```

```python
import jax
import jax.numpy as jnp
from jax import lax
from jax.experimental import pallas as pl
from jax.experimental.pallas import tpu as pltpu
from jax.sharding import PartitionSpec as P

TILE = 128
SUPERS = 3
SAMPLES = 2048
TILES_SUP = 16
TILES = 48
MAX_BELOW = 32
NX, NY, NZ = 4, 4, 8
ROWS = 128
HALF = 64
MESH = pl.DeviceIdType.MESH
F32 = jnp.float32
BF16 = jnp.bfloat16


def split(v):
    hi = v.astype(BF16)
    return hi, (v - hi.astype(F32)).astype(BF16)


def kernel(
    home_in, rows_in, counts_in, rhs, below, diag, out,
    home, rows_ref, counts, mask,
    b8, df0, df1, lf0, lf1, dhi, dlo, lhi, llo, xd, xl,
    part, rbuf, chunk, res, spart, exch, sol, outs, outr,
    send, recv, local,
):
    blk, col = lax.axis_index("blk"), lax.axis_index("col")
    y, z = blk // NZ, blk % NZ
    x, k = col // 2, col % 2
    count = [0, 0]

    def at(dy=0, dz=0, dx=0, dk=0):
        return (((y + dy) % NY) * NZ + (z + dz) % NZ, ((x + dx) % NX) * 2 + (k + dk) % 2)

    def push(src, dst, slot=None, **where):
        i = slot
        if slot is None:
            i = count[0]
            count[0] += 1
        c = pltpu.make_async_remote_copy(
            src_ref=src, dst_ref=dst, send_sem=send.at[i], recv_sem=recv.at[i],
            device_id=at(**where), device_id_type=MESH,
        )
        c.start()
        if slot is None:
            sent.append(c)
        return c

    def keep(src, dst):
        i = count[1]
        count[1] += 1
        c = pltpu.make_async_copy(src, dst, local.at[i])
        c.start()
        return c

    sent = []
    ints = [keep(home_in, home), keep(rows_in, rows_ref), keep(counts_in, counts)]
    own = [keep(diag.at[0], df0.at[y, x]), keep(diag.at[1], df1.at[x, y])]
    own_b = []
    for h in range(2):
        start = pl.multiple_of((2 * x + h) * 256 + y * HALF, HALF)
        own_b.append(keep(rhs.at[:, pl.ds(start, HALF), :], b8.at[y, :, pl.ds(h * HALF, HALF), :]))
    own_l = []
    for s in (1, 0):
        own_l.append(
            [keep(below.at[0, s], lf0.at[s, y, x]), keep(below.at[1, s], lf1.at[s, x, y])]
        )

    peers = [dict(dy=d) for d in range(1, NY)] + [dict(dx=d) for d in range(1, NX)]
    peers += [dict(dz=d) for d in range(1, NZ)] + [dict(dk=1)] + [dict(dy=d, dk=1) for d in range(1, NY)]
    barrier = pltpu.get_barrier_semaphore()
    for p in peers:
        pl.semaphore_signal(barrier, inc=1, device_id=at(**p), device_id_type=MESH)
    pl.semaphore_wait(barrier, len(peers))

    half = pl.ds(pl.multiple_of(k * HALF, HALF), HALF)
    bcopies = []
    for d in (1, 3, 2):
        start = pl.multiple_of((2 * x + k) * 256 + ((y + d) % NY) * HALF, HALF)
        bcopies.append(push(rhs.at[:, pl.ds(start, HALF), :], b8.at[y, :, half, :], dy=d))

    def begin(a0, a1, own0, own1):
        hop = {}
        for d in (1, 3, 2):
            hop["x", d] = push(own0, a0.at[y, x], dx=d)
            hop["y", d] = push(own1, a1.at[x, y], dy=d)
        for d in (1, 3):
            hop["yy", d, 0] = push(own0, a0.at[y, x], dy=d)
            hop["xx", d, 0] = push(own1, a1.at[x, y], dx=d)
        return a0, a1, hop

    def forward(st):
        a0, a1, hop = st
        for e in (1, 3, 2):
            hop.pop(("x", e)).wait_recv()
            piece = a0.at[y, (x - e) % NX]
            for d in (1, 3):
                hop["yy", d, e] = push(piece, piece, dy=d)
            hop.pop(("y", e)).wait_recv()
            piece = a1.at[x, (y - e) % NY]
            for d in (1, 3):
                hop["xx", d, e] = push(piece, piece, dx=d)

    def relay(st):
        a0, a1, hop = st
        for i in range(2):
            for d, e in ((1, (0, 1)[i]), (3, (3, 2)[i])):
                hop.pop(("yy", d, e)).wait_recv()
                piece = a0.at[(y - d) % NY, (x - e) % NX]
                hop["far y", d, e] = push(piece, piece, dy=d)
                hop.pop(("xx", d, e)).wait_recv()
                piece = a1.at[(x - d) % NX, (y - e) % NY]
                hop["far x", d, e] = push(piece, piece, dx=d)

    def finish(st):
        for c in st[2].values():
            c.wait_recv()

    def arrive(cs):
        for c in cs:
            c.wait_recv()

    sd = begin(df0, df1, diag.at[0], diag.at[1])

    slots = [((i // 2) * NZ + z) * 2 + i % 2 for i in range(8)]

    def find(r, tiles):
        h = home[r]
        return tuple(jnp.where(h == slots[i], r, tiles[i]) for i in range(8))

    for c in ints:
        c.wait()
    tiles = lax.fori_loop(0, TILES, find, (jnp.int32(-1),) * 8, unroll=4)
    for s in range(SUPERS):
        used = counts[s]

        def hit(e, found):
            r = jnp.where(e < used, rows_ref[s, e], -2)
            return tuple(jnp.where(r == tiles[i], 1.0, found[i]) for i in range(8))

        found = lax.fori_loop(0, MAX_BELOW, hit, (jnp.float32(0.0),) * 8, unroll=4)
        for i in range(8):
            q = tiles[i] - s * TILES_SUP
            inside = (q >= 0) & (q < TILES_SUP)
            mask[(s * 10 + 8) * 8 + i] = jnp.where(inside, 1.0, 0.0)
            mask[(s * 10 + 9) * 8 + i] = found[i]
            for t in range(8):
                col_tile = 4 * (t // 2) + 2 * k + t % 2
                mask[(s * 10 + t) * 8 + i] = jnp.where(q == col_tile, 1.0, 0.0)

    forward(sd)
    s1 = begin(lf0.at[1], lf1.at[1], below.at[0, 1], below.at[1, 1])
    for c in own_b:
        c.wait()
    swaps = []
    for d, c in zip((1, 3, 2), bcopies):
        c.wait_recv()
        piece = b8.at[(y - d) % NY, :, half, :]
        swaps.append(push(piece, piece, dk=1))
    arrive(swaps)

    def place(s):
        def tile(t, carry):
            acc = jnp.zeros((ROWS, TILE), F32)
            for i in range(8):
                acc = acc + b8[i // 2, i % 2] * mask[(s * 10 + t) * 8 + i]
            part[s, 0, t] = acc[:HALF]
            part[s, 1, t] = acc[HALF:]
            return carry

        lax.fori_loop(0, 8, tile, 0)

    def scatter(s, h):
        cs = []
        for d in (4, 3, 5, 2, 6, 1, 7):
            cs.append(push(part.at[s, h, (z + d) % NZ], rbuf.at[s, h, d - 1], dz=d))
        return cs

    def turn(s, h, cs):
        arrive(cs)
        total = part[s, h, z]
        for d in range(1, NZ):
            total = total + rbuf[s, h, d - 1]
        chunk[s, h] = total
        res[s, h, z] = total
        return [push(chunk.at[s, h], res.at[s, h, z], dz=d) for d in (4, 3, 5, 2, 6, 1, 7)]

    place(2)
    rs = [scatter(2, 0), scatter(2, 1)]
    relay(sd)
    forward(s1)
    place(1)
    place(0)
    ag = [turn(2, h, rs[h]) for h in range(2)]
    for c in own:
        c.wait()
    finish(sd)

    def convert_d(i, carry):
        a, b = i // 4, i % 4
        rows = pl.ds(pl.multiple_of(b * 256, 256), 256)
        for j, v in ((0, df0[a, b]), (1, df1[b, a])):
            hi, lo = split(v)
            dhi[a, rows, j * TILE:(j + 1) * TILE] = hi
            dlo[a, rows, j * TILE:(j + 1) * TILE] = lo
        return carry

    def convert_l(s):
        def step(i, carry):
            a, b = i // 4, i % 4
            for j, v in ((0, lf0[s, a, b]), (1, lf1[s, b, a])):
                hi, lo = split(v)
                rows = pl.ds(pl.multiple_of(a * 256 + j * TILE, TILE), TILE)
                lhi[b, rows, :] = hi
                llo[b, rows, :] = lo
            return carry

        lax.fori_loop(0, 16, step, 0)

    def product(xs, whi, wlo, n):
        both = jnp.dot(xs[...], whi[n], preferred_element_type=F32)
        cross = jnp.dot(xs[:HALF], wlo[n], preferred_element_type=F32)
        return both[:HALF] + (both[HALF:] + cross)

    def fill(s, h, cs):
        arrive(cs)
        for t in range(8):
            hi, lo = split(res[s, h, t])
            xd[:HALF, t * TILE:(t + 1) * TILE] = hi
            xd[HALF:, t * TILE:(t + 1) * TILE] = lo

    def diag_step(s, h, cs):
        fill(s, h, cs)
        base = count[0]
        count[0] += 4

        def step(n, carry):
            spart[s, h, n] = product(xd, dhi, dlo, n)
            trade(s, h, n, base).start()
            return carry

        lax.fori_loop(0, 4, step, 0)
        return base

    def trade(s, h, n, base):
        return pltpu.make_async_remote_copy(
            src_ref=spart.at[s, h, n], dst_ref=exch.at[s, h, n],
            send_sem=send.at[base + n], recv_sem=recv.at[base + n],
            device_id=at(dk=1), device_id_type=MESH,
        )

    def lanes(s, row, n):
        lane = lax.broadcasted_iota(jnp.int32, (1, 256), 1)
        base = (s * 10 + row) * 8 + 2 * n
        return jnp.where(lane < TILE, mask[base], mask[base + 1])

    def below_step(s, h, ex):
        def weigh(n, carry):
            trade(s + 1, h, n, ex).wait()
            v = spart[s + 1, h, n] + exch[s + 1, h, n]
            v = jnp.where(lanes(s + 1, 8, n) > 0.5, v, 0.0)
            if s == 0:
                v = v + sol[h, n]
            sol[h, n] = v
            hi, lo = split(v * lanes(s, 9, n))
            where = pl.ds(pl.multiple_of(n * 256, 256), 256)
            xl[:HALF, where] = hi
            xl[HALF:, where] = lo
            return carry

        lax.fori_loop(0, 4, weigh, 0)

        base = count[0]
        count[0] += NZ

        def tile(t, d):
            return pltpu.make_async_remote_copy(
                src_ref=part.at[s, h, t], dst_ref=rbuf.at[s, h, d - 1],
                send_sem=send.at[base + d], recv_sem=recv.at[base + d],
                device_id=(y * NZ + t, col), device_id_type=MESH,
            )

        def step(i, carry):
            n = (z // 2 + 2 + i) % 4
            acc = product(xl, lhi, llo, n)
            for j in range(2):
                t = 2 * n + j
                part[s, h, t] = part[s, h, t] - acc[:, j * TILE:(j + 1) * TILE]

                @pl.when(t != z)
                def _():
                    tile(t, (t - z + NZ) % NZ).start()

            return carry

        lax.fori_loop(0, 4, step, 0)
        cs = [tile((z + d) % NZ, d) for d in range(1, NZ)]
        sent.extend(cs)
        return cs

    lax.fori_loop(0, 16, convert_d, 0)
    relay(s1)
    ex = [diag_step(2, h, ag[h]) for h in range(2)]
    s0 = begin(lf0.at[0], lf1.at[0], below.at[0, 0], below.at[1, 0])
    for c in own_l:
        for w in c:
            w.wait()
    finish(s1)
    convert_l(1)
    rs = [below_step(1, h, ex[h]) for h in range(2)]
    forward(s0)
    ag = [turn(1, h, rs[h]) for h in range(2)]
    relay(s0)
    ex0 = diag_step(1, 0, ag[0])
    finish(s0)
    convert_l(0)
    rs0 = below_step(0, 0, ex0)
    ex1 = diag_step(1, 1, ag[1])
    rs1 = below_step(0, 1, ex1)
    ag = [turn(0, 0, rs0), turn(0, 1, rs1)]
    base = count[0]
    count[0] += 16

    def last(h, d):
        rel = (h + k) % 2
        return pltpu.make_async_remote_copy(
            src_ref=outs.at[h, (y + d) % NY], dst_ref=outr.at[rel, y],
            send_sem=send.at[base + 4 * h + d], recv_sem=recv.at[base + 8 + 4 * rel + d],
            device_id=(((y + d) % NY) * NZ + z, x * 2 + h), device_id_type=MESH,
        )

    def landed(rel, d):
        return pltpu.make_async_remote_copy(
            src_ref=outs.at[0, y], dst_ref=outr.at[rel, (y - d) % NY],
            send_sem=send.at[base + 8 + 4 * rel + d], recv_sem=recv.at[base + 8 + 4 * rel + d],
            device_id=at(dy=d, dk=rel), device_id_type=MESH,
        )

    for h in range(2):
        fill(0, h, ag[h])

        def closing(n, carry):
            v = jnp.where(lanes(0, 8, n) > 0.5, product(xd, dhi, dlo, n), 0.0)
            mine = jnp.full((1, 256), jnp.where(k == h, 1.0, 0.0), F32) > 0.5
            outs[h, n] = v + jnp.where(mine, sol[h, n], 0.0)
            return carry

        lax.fori_loop(0, 4, closing, 0)
        for d in (1, 3, 2):
            last(h, d).start()

        @pl.when(k != h)
        def _():
            last(h, 0).start()

    outr[0, y] = outs[k, y]
    for rel in range(2):
        for d in (1, 3, 2, 0):
            if rel or d:
                landed(rel, d).wait_recv()
    for n in range(4):
        v = outr[0, n] + outr[1, n]
        for j in range(2):
            out[j, n * HALF:(n + 1) * HALF, :] = v[:, j * TILE:(j + 1) * TILE]
    for h in range(2):
        for d in (1, 3, 2):
            last(h, d).wait_send()

        @pl.when(k != h)
        def _():
            last(h, 0).wait_send()

    for c in sent:
        c.wait_send()


COPIES = 240


def body(right_side, below_blocks, diag_cols, tile_home, block_rows, block_counts):
    vm = pltpu.VMEM
    hbm = pl.BlockSpec(memory_space=pltpu.HBM)
    return pl.pallas_call(
        kernel,
        name="solve",
        out_shape=jax.ShapeDtypeStruct((2, 256, TILE), F32),
        in_specs=[hbm] * 6,
        out_specs=pl.BlockSpec(memory_space=pltpu.VMEM),
        scratch_shapes=[
            pltpu.SMEM((TILES,), jnp.int32),
            pltpu.SMEM((SUPERS, MAX_BELOW), jnp.int32),
            pltpu.SMEM((SUPERS,), jnp.int32),
            pltpu.SMEM((SUPERS * 10 * 8,), F32),
            vm((4, 2, ROWS, TILE), F32),
            vm((4, 4, 256, TILE), F32),
            vm((4, 4, 256, TILE), F32),
            vm((2, 4, 4, TILE, 256), F32),
            vm((2, 4, 4, TILE, 256), F32),
            vm((4, 1024, 256), BF16),
            vm((4, 1024, 256), BF16),
            vm((4, 1024, 256), BF16),
            vm((4, 1024, 256), BF16),
            vm((ROWS, 1024), BF16),
            vm((ROWS, 1024), BF16),
            vm((3, 2, 8, HALF, TILE), F32),
            vm((3, 2, 7, HALF, TILE), F32),
            vm((3, 2, HALF, TILE), F32),
            vm((3, 2, 8, HALF, TILE), F32),
            vm((3, 2, 4, HALF, 256), F32),
            vm((3, 2, 4, HALF, 256), F32),
            vm((2, 4, HALF, 256), F32),
            vm((2, 4, HALF, 256), F32),
            vm((2, 4, HALF, 256), F32),
            pltpu.SemaphoreType.DMA((COPIES,)),
            pltpu.SemaphoreType.DMA((COPIES,)),
            pltpu.SemaphoreType.DMA((12,)),
        ],
        compiler_params=pltpu.CompilerParams(
            collective_id=0, has_side_effects=True, vmem_limit_bytes=60 * 2**20
        ),
    )(tile_home, block_rows, block_counts, right_side, below_blocks, diag_cols)


def solution(mesh):
    return jax.shard_map(
        body,
        mesh=mesh,
        in_specs=(
            P("blk", None, None),
            P("blk", None, None, "col"),
            P("blk", "col", None),
            P(),
            P(),
            P(),
        ),
        out_specs=P("blk", "col", None),
        check_vma=False,
    )
```

```python
import jax
import jax.numpy as jnp
from jax import lax
from jax.experimental import pallas as pl
from jax.experimental.pallas import tpu as pltpu
from jax.sharding import PartitionSpec as P

TILE = 128
SUPERS = 3
SAMPLES = 2048
TILES_SUP = 16
TILES = 48
MAX_BELOW = 32
NX, NY, NZ = 4, 4, 8
ROWS = 128
HALF = 64
MESH = pl.DeviceIdType.MESH
F32 = jnp.float32
BF16 = jnp.bfloat16


def split(v):
    hi = v.astype(BF16)
    return hi, (v - hi.astype(F32)).astype(BF16)


def kernel(
    home_in, rows_in, counts_in, rhs, below, diag, out,
    home, rows_ref, counts, mask,
    b8, df0, df1, lf0, lf1, dhi, dlo, lhi, llo, xd, xl,
    part, rbuf, chunk, res, spart, exch, sol, outs, outr,
    send, recv, local,
):
    blk, col = lax.axis_index("blk"), lax.axis_index("col")
    y, z = blk // NZ, blk % NZ
    x, k = col // 2, col % 2
    count = [0, 0]

    def at(dy=0, dz=0, dx=0, dk=0):
        return (((y + dy) % NY) * NZ + (z + dz) % NZ, ((x + dx) % NX) * 2 + (k + dk) % 2)

    def push(src, dst, slot=None, **where):
        i = slot
        if slot is None:
            i = count[0]
            count[0] += 1
        c = pltpu.make_async_remote_copy(
            src_ref=src, dst_ref=dst, send_sem=send.at[i], recv_sem=recv.at[i],
            device_id=at(**where), device_id_type=MESH,
        )
        c.start()
        if slot is None:
            sent.append(c)
        return c

    def keep(src, dst):
        i = count[1]
        count[1] += 1
        c = pltpu.make_async_copy(src, dst, local.at[i])
        c.start()
        return c

    sent = []
    ints = [keep(home_in, home), keep(rows_in, rows_ref), keep(counts_in, counts)]
    own = [keep(diag.at[0], df0.at[y, x]), keep(diag.at[1], df1.at[x, y])]
    own_b = []
    for h in range(2):
        start = pl.multiple_of((2 * x + h) * 256 + y * HALF, HALF)
        own_b.append(keep(rhs.at[:, pl.ds(start, HALF), :], b8.at[y, :, pl.ds(h * HALF, HALF), :]))
    own_l = []
    for s in (1, 0):
        own_l.append(
            [keep(below.at[0, s], lf0.at[s, y, x]), keep(below.at[1, s], lf1.at[s, x, y])]
        )

    peers = [dict(dy=d) for d in range(1, NY)] + [dict(dx=d) for d in range(1, NX)]
    peers += [dict(dz=d) for d in range(1, NZ)] + [dict(dk=1)] + [dict(dy=d, dk=1) for d in range(1, NY)]
    barrier = pltpu.get_barrier_semaphore()
    for p in peers:
        pl.semaphore_signal(barrier, inc=1, device_id=at(**p), device_id_type=MESH)
    pl.semaphore_wait(barrier, len(peers))

    half = pl.ds(pl.multiple_of(k * HALF, HALF), HALF)
    bcopies = []
    for d in (1, 3, 2):
        start = pl.multiple_of((2 * x + k) * 256 + ((y + d) % NY) * HALF, HALF)
        bcopies.append(push(rhs.at[:, pl.ds(start, HALF), :], b8.at[y, :, half, :], dy=d))

    def begin(a0, a1, own0, own1):
        hop = {}
        for d in (1, 3, 2):
            hop["x", d] = push(own0, a0.at[y, x], dx=d)
            hop["y", d] = push(own1, a1.at[x, y], dy=d)
        for d in (1, 3):
            hop["yy", d, 0] = push(own0, a0.at[y, x], dy=d)
            hop["xx", d, 0] = push(own1, a1.at[x, y], dx=d)
        return a0, a1, hop

    def forward(st):
        a0, a1, hop = st
        for e in (1, 3, 2):
            hop.pop(("x", e)).wait_recv()
            piece = a0.at[y, (x - e) % NX]
            for d in (1, 3):
                hop["yy", d, e] = push(piece, piece, dy=d)
            hop.pop(("y", e)).wait_recv()
            piece = a1.at[x, (y - e) % NY]
            for d in (1, 3):
                hop["xx", d, e] = push(piece, piece, dx=d)

    def relay(st):
        a0, a1, hop = st
        for i in range(2):
            for d, e in ((1, (0, 1)[i]), (3, (3, 2)[i])):
                hop.pop(("yy", d, e)).wait_recv()
                piece = a0.at[(y - d) % NY, (x - e) % NX]
                hop["far y", d, e] = push(piece, piece, dy=d)
                hop.pop(("xx", d, e)).wait_recv()
                piece = a1.at[(x - d) % NX, (y - e) % NY]
                hop["far x", d, e] = push(piece, piece, dx=d)

    def near(st):
        hop = st[2]
        for key in [key for key in hop if key[0] in ("yy", "xx")]:
            hop.pop(key).wait_recv()

    def finish(st):
        for c in st[2].values():
            c.wait_recv()

    def arrive(cs):
        for c in cs:
            c.wait_recv()

    sd = begin(df0, df1, diag.at[0], diag.at[1])

    slots = [((i // 2) * NZ + z) * 2 + i % 2 for i in range(8)]

    def find(r, tiles):
        h = home[r]
        return tuple(jnp.where(h == slots[i], r, tiles[i]) for i in range(8))

    for c in ints:
        c.wait()
    tiles = lax.fori_loop(0, TILES, find, (jnp.int32(-1),) * 8, unroll=4)
    for s in range(SUPERS):
        used = counts[s]

        def hit(e, found):
            r = jnp.where(e < used, rows_ref[s, e], -2)
            return tuple(jnp.where(r == tiles[i], 1.0, found[i]) for i in range(8))

        found = lax.fori_loop(0, MAX_BELOW, hit, (jnp.float32(0.0),) * 8, unroll=4)
        for i in range(8):
            q = tiles[i] - s * TILES_SUP
            inside = (q >= 0) & (q < TILES_SUP)
            mask[(s * 10 + 8) * 8 + i] = jnp.where(inside, 1.0, 0.0)
            mask[(s * 10 + 9) * 8 + i] = found[i]
            for t in range(8):
                col_tile = 4 * (t // 2) + 2 * k + t % 2
                mask[(s * 10 + t) * 8 + i] = jnp.where(q == col_tile, 1.0, 0.0)

    forward(sd)
    s1 = begin(lf0.at[1], lf1.at[1], below.at[0, 1], below.at[1, 1])
    for c in own_b:
        c.wait()
    swaps = []
    for d, c in zip((1, 3, 2), bcopies):
        c.wait_recv()
        piece = b8.at[(y - d) % NY, :, half, :]
        swaps.append(push(piece, piece, dk=1))
    arrive(swaps)

    def place(s):
        def tile(t, carry):
            acc = jnp.zeros((ROWS, TILE), F32)
            for i in range(8):
                acc = acc + b8[i // 2, i % 2] * mask[(s * 10 + t) * 8 + i]
            part[s, 0, t] = acc[:HALF]
            part[s, 1, t] = acc[HALF:]
            return carry

        lax.fori_loop(0, 8, tile, 0)

    def scatter(s, h):
        cs = []
        for d in (4, 3, 5, 2, 6, 1, 7):
            cs.append(push(part.at[s, h, (z + d) % NZ], rbuf.at[s, h, d - 1], dz=d))
        return cs

    def turn(s, h, cs):
        arrive(cs)
        total = part[s, h, z]
        for d in range(1, NZ):
            total = total + rbuf[s, h, d - 1]
        chunk[s, h] = total
        res[s, h, z] = total
        return [push(chunk.at[s, h], res.at[s, h, z], dz=d) for d in (4, 3, 5, 2, 6, 1, 7)]

    place(2)
    rs = [scatter(2, 0), scatter(2, 1)]
    relay(sd)
    forward(s1)
    place(1)
    place(0)
    ag = [turn(2, h, rs[h]) for h in range(2)]
    for c in own:
        c.wait()
    finish(sd)

    def convert_d(i, carry):
        a, b = i // 4, i % 4
        rows = pl.ds(pl.multiple_of(b * 256, 256), 256)
        for j, v in ((0, df0[a, b]), (1, df1[b, a])):
            hi, lo = split(v)
            dhi[a, rows, j * TILE:(j + 1) * TILE] = hi
            dlo[a, rows, j * TILE:(j + 1) * TILE] = lo
        return carry

    def convert_l(s, first, steps):
        def step(i, carry):
            far, same = first + i // 4, i % 4
            for j, a, b in ((0, (y + far) % NY, same), (1, same, (x + far) % NX)):
                hi, lo = split(lf1[s, b, a] if j else lf0[s, a, b])
                rows = pl.ds(pl.multiple_of(a * 256 + j * TILE, TILE), TILE)
                lhi[b, rows, :] = hi
                llo[b, rows, :] = lo
            return carry

        lax.fori_loop(0, steps, step, 0)

    def product(xs, whi, wlo, n):
        both = jnp.dot(xs[...], whi[n], preferred_element_type=F32)
        cross = jnp.dot(xs[:HALF], wlo[n], preferred_element_type=F32)
        return both[:HALF] + (both[HALF:] + cross)

    def fill(s, h, cs):
        arrive(cs)
        for t in range(8):
            hi, lo = split(res[s, h, t])
            xd[:HALF, t * TILE:(t + 1) * TILE] = hi
            xd[HALF:, t * TILE:(t + 1) * TILE] = lo

    def diag_step(s, h, cs):
        fill(s, h, cs)
        base = count[0]
        count[0] += 4

        def step(n, carry):
            spart[s, h, n] = product(xd, dhi, dlo, n)
            trade(s, h, n, base).start()
            return carry

        lax.fori_loop(0, 4, step, 0)
        return base

    def trade(s, h, n, base):
        return pltpu.make_async_remote_copy(
            src_ref=spart.at[s, h, n], dst_ref=exch.at[s, h, n],
            send_sem=send.at[base + n], recv_sem=recv.at[base + n],
            device_id=at(dk=1), device_id_type=MESH,
        )

    def lanes(s, row, n):
        lane = lax.broadcasted_iota(jnp.int32, (1, 256), 1)
        base = (s * 10 + row) * 8 + 2 * n
        return jnp.where(lane < TILE, mask[base], mask[base + 1])

    def below_step(s, h, ex):
        def weigh(n, carry):
            trade(s + 1, h, n, ex).wait()
            v = spart[s + 1, h, n] + exch[s + 1, h, n]
            v = jnp.where(lanes(s + 1, 8, n) > 0.5, v, 0.0)
            if s == 0:
                v = v + sol[h, n]
            sol[h, n] = v
            hi, lo = split(v * lanes(s, 9, n))
            where = pl.ds(pl.multiple_of(n * 256, 256), 256)
            xl[:HALF, where] = hi
            xl[HALF:, where] = lo
            return carry

        lax.fori_loop(0, 4, weigh, 0)

        base = count[0]
        count[0] += NZ

        def tile(t, d):
            return pltpu.make_async_remote_copy(
                src_ref=part.at[s, h, t], dst_ref=rbuf.at[s, h, d - 1],
                send_sem=send.at[base + d], recv_sem=recv.at[base + d],
                device_id=(y * NZ + t, col), device_id_type=MESH,
            )

        def step(i, carry):
            n = (z // 2 + 2 + i) % 4
            acc = product(xl, lhi, llo, n)
            for j in range(2):
                t = 2 * n + j
                part[s, h, t] = part[s, h, t] - acc[:, j * TILE:(j + 1) * TILE]

                @pl.when(t != z)
                def _():
                    tile(t, (t - z + NZ) % NZ).start()

            return carry

        lax.fori_loop(0, 4, step, 0)
        cs = [tile((z + d) % NZ, d) for d in range(1, NZ)]
        sent.extend(cs)
        return cs

    lax.fori_loop(0, 16, convert_d, 0)
    relay(s1)
    ex = [diag_step(2, h, ag[h]) for h in range(2)]
    s0 = begin(lf0.at[0], lf1.at[0], below.at[0, 0], below.at[1, 0])
    for c in own_l:
        for w in c:
            w.wait()
    near(s1)
    convert_l(1, 3, 12)
    finish(s1)
    convert_l(1, 2, 4)
    rs = [below_step(1, h, ex[h]) for h in range(2)]
    forward(s0)
    ag = [turn(1, h, rs[h]) for h in range(2)]
    relay(s0)
    near(s0)
    convert_l(0, 3, 12)
    ex0 = diag_step(1, 0, ag[0])
    finish(s0)
    convert_l(0, 2, 4)
    rs0 = below_step(0, 0, ex0)
    ex1 = diag_step(1, 1, ag[1])
    rs1 = below_step(0, 1, ex1)
    ag = [turn(0, 0, rs0), turn(0, 1, rs1)]
    base = count[0]
    count[0] += 16

    def last(h, d):
        rel = (h + k) % 2
        return pltpu.make_async_remote_copy(
            src_ref=outs.at[h, (y + d) % NY], dst_ref=outr.at[rel, y],
            send_sem=send.at[base + 4 * h + d], recv_sem=recv.at[base + 8 + 4 * rel + d],
            device_id=(((y + d) % NY) * NZ + z, x * 2 + h), device_id_type=MESH,
        )

    def landed(rel, d):
        return pltpu.make_async_remote_copy(
            src_ref=outs.at[0, y], dst_ref=outr.at[rel, (y - d) % NY],
            send_sem=send.at[base + 8 + 4 * rel + d], recv_sem=recv.at[base + 8 + 4 * rel + d],
            device_id=at(dy=d, dk=rel), device_id_type=MESH,
        )

    for h in range(2):
        fill(0, h, ag[h])

        def closing(n, carry):
            v = jnp.where(lanes(0, 8, n) > 0.5, product(xd, dhi, dlo, n), 0.0)
            mine = jnp.full((1, 256), jnp.where(k == h, 1.0, 0.0), F32) > 0.5
            outs[h, n] = v + jnp.where(mine, sol[h, n], 0.0)
            return carry

        lax.fori_loop(0, 4, closing, 0)
        for d in (1, 3, 2):
            last(h, d).start()

        @pl.when(k != h)
        def _():
            last(h, 0).start()

    outr[0, y] = outs[k, y]
    for rel in range(2):
        for d in (1, 3, 2, 0):
            if rel or d:
                landed(rel, d).wait_recv()
    for n in range(4):
        v = outr[0, n] + outr[1, n]
        for j in range(2):
            out[j, n * HALF:(n + 1) * HALF, :] = v[:, j * TILE:(j + 1) * TILE]
    for h in range(2):
        for d in (1, 3, 2):
            last(h, d).wait_send()

        @pl.when(k != h)
        def _():
            last(h, 0).wait_send()

    for c in sent:
        c.wait_send()


COPIES = 240


def body(right_side, below_blocks, diag_cols, tile_home, block_rows, block_counts):
    vm = pltpu.VMEM
    hbm = pl.BlockSpec(memory_space=pltpu.HBM)
    return pl.pallas_call(
        kernel,
        name="solve",
        out_shape=jax.ShapeDtypeStruct((2, 256, TILE), F32),
        in_specs=[hbm] * 6,
        out_specs=pl.BlockSpec(memory_space=pltpu.VMEM),
        scratch_shapes=[
            pltpu.SMEM((TILES,), jnp.int32),
            pltpu.SMEM((SUPERS, MAX_BELOW), jnp.int32),
            pltpu.SMEM((SUPERS,), jnp.int32),
            pltpu.SMEM((SUPERS * 10 * 8,), F32),
            vm((4, 2, ROWS, TILE), F32),
            vm((4, 4, 256, TILE), F32),
            vm((4, 4, 256, TILE), F32),
            vm((2, 4, 4, TILE, 256), F32),
            vm((2, 4, 4, TILE, 256), F32),
            vm((4, 1024, 256), BF16),
            vm((4, 1024, 256), BF16),
            vm((4, 1024, 256), BF16),
            vm((4, 1024, 256), BF16),
            vm((ROWS, 1024), BF16),
            vm((ROWS, 1024), BF16),
            vm((3, 2, 8, HALF, TILE), F32),
            vm((3, 2, 7, HALF, TILE), F32),
            vm((3, 2, HALF, TILE), F32),
            vm((3, 2, 8, HALF, TILE), F32),
            vm((3, 2, 4, HALF, 256), F32),
            vm((3, 2, 4, HALF, 256), F32),
            vm((2, 4, HALF, 256), F32),
            vm((2, 4, HALF, 256), F32),
            vm((2, 4, HALF, 256), F32),
            pltpu.SemaphoreType.DMA((COPIES,)),
            pltpu.SemaphoreType.DMA((COPIES,)),
            pltpu.SemaphoreType.DMA((12,)),
        ],
        compiler_params=pltpu.CompilerParams(
            collective_id=0, has_side_effects=True, vmem_limit_bytes=60 * 2**20
        ),
    )(tile_home, block_rows, block_counts, right_side, below_blocks, diag_cols)


def solution(mesh):
    return jax.shard_map(
        body,
        mesh=mesh,
        in_specs=(
            P("blk", None, None),
            P("blk", None, None, "col"),
            P("blk", "col", None),
            P(),
            P(),
            P(),
        ),
        out_specs=P("blk", "col", None),
        check_vma=False,
    )
```
